32 devices in a mesh: fsdp: 8 (over z, x), ctx: 4 (over y, core).
Axes of the slice: x: 2, y: 2, z: 4, core: 2. Of those that a mesh axis runs over, the one named last changes fastest.
Arguments:
- hidden_in: bfloat16 [2, 8, 256, 1024], P(None, 'fsdp', 'ctx'), may hold values from -6 to 6
- segment_ids: int32 [2, 8, 256], P(None, 'fsdp'), may hold values from 0 to 16, as said below
- out_grad: bfloat16 [2, 8, 256, 1024], P(None, 'fsdp', 'ctx'), may hold values from -6 to 6
- norm_gain: bfloat16 [1024], P('fsdp'), may hold values from 0.099609375 to 1.8984375
- w_qkv: bfloat16 [1024, 768], P('fsdp'), may hold values from -0.1875 to 0.1875
- w_o: bfloat16 [512, 1024], P('fsdp'), may hold values from -1 to 1
- w_zx: bfloat16 [1024, 3072], P('fsdp'), may hold values from -0.1875 to 0.1875
- w_bc: bfloat16 [1024, 256], P('fsdp'), may hold values from -0.1875 to 0.1875
- w_dt: bfloat16 [1024, 24], P('fsdp'), may hold values from -0.1875 to 0.1875
- conv_w: bfloat16 [4, 1792], P(None, 'fsdp'), may hold values from -3 to 3
- conv_b: bfloat16 [1792], P('fsdp'), may hold values from -3 to 3
- dt_bias: float32 [24], replicated, may hold values from -6.5 to -4.5
- a_log: float32 [24], replicated, may hold values from -2.5 to 2
- d_skip: float32 [24], replicated, may hold values from 0.5 to 1.5
- w_out: bfloat16 [1536, 1024], P('fsdp'), may hold values from -0.15625 to 0.15625
- second_gain: bfloat16 [1024], P('fsdp'), may hold values from 0.099609375 to 1.8984375
- w_gate_up: bfloat16 [1024, 4096], P('fsdp'), may hold values from -0.1875 to 0.1875
- w_down: bfloat16 [2048, 1024], P('fsdp'), may hold values from -0.1875 to 0.1875
Outputs:
- block_out: bfloat16 [2, 8, 256, 1024], P(None, 'fsdp', 'ctx')
- grad_in: bfloat16 [2, 8, 256, 1024], P(None, 'fsdp', 'ctx')
- grad_gain: float32 [1024], P('fsdp')
- grad_qkv: float32 [1024, 768], P('fsdp')
- grad_o: float32 [512, 1024], P('fsdp')
- grad_zx: float32 [1024, 3072], P('fsdp')
- grad_bc: float32 [1024, 256], P('fsdp')
- grad_dt: float32 [1024, 24], P('fsdp')
- grad_conv_w: float32 [4, 1792], P(None, 'fsdp')
- grad_conv_b: float32 [1792], P('fsdp')
- grad_dt_bias: float32 [24], replicated
- grad_a_log: float32 [24], replicated
- grad_d_skip: float32 [24], replicated
- grad_out: float32 [1536, 1024], P('fsdp')
- grad_second_gain: float32 [1024], P('fsdp')
- grad_gate_up: float32 [1024, 4096], P('fsdp')
- grad_down: float32 [2048, 1024], P('fsdp')
The draws below stay inside these ranges and needn't reach their ends.
Inputs may be any that keep to these rules, and one draw needn't show every extreme that they name: `segment_ids`: in each pack the ids start at 0 at position 0, never fall, and rise by at most one from a token to the next; each pack holds exactly 17 segments; one segment covers every position from 32 to 223.
All inputs are finite; a program needn't handle non-finite values.
Results may differ from the reference program's by a relative error of at most 0.023.
Values may be sent and summed in bfloat16 or wider, within the bound.
No kernel may reach another device: no remote copies, remote signals or barrier semaphores. Data moves between devices by JAX's collectives and lax.ppermute only.
A program may use at most 192 MiB of HBM per device.

```python
import math
from functools import partial
import jax
import jax.numpy as jnp
from jax import lax

D = 1024
HEADS = 8
KV = 2
HD = 64
MH = 24
MP = 64
NS = 128
CONV = 4
FF = 2048
CT = 64
MICRO = 2
PACKS = 8
SEQ = 256
QW = 512
KW = 128
DI = 1536
XC = 1792


def draw_segment_ids(key, part):
    key = jax.random.fold_in(key, 11)
    positions = jnp.arange(SEQ).astype(jnp.int32)
    edge = CT // 2
    allowed = (positions >= 1) & ((positions < edge) | (positions >= SEQ - edge))
    picks = jax.random.randint(key, (MICRO, PACKS, SEQ), 0, 2 ** 18).astype(jnp.int32)
    scores = jnp.where(allowed[None, None, :], picks * SEQ + positions[None, None, :], 2 ** 30).astype(jnp.int32)
    order = jnp.argsort(scores, axis=-1, stable=True)
    ranks = jnp.argsort(order, axis=-1, stable=True)
    flags = (ranks < CT // 4).astype(jnp.int32)
    return jnp.cumsum(flags, axis=-1).astype(jnp.int32)


def draw_a_log(key, part):
    key = jax.random.fold_in(key, 23)
    values = jax.random.uniform(key, (MH,), jnp.float32, -1.5, 2.0)
    return values.astype(jnp.float32)


def shard_levels(rng, dims, shards, least, high):
    gain = 1.0
    for axis_at, parts in shards:
        heights = jax.random.uniform(jax.random.fold_in(jax.random.fold_in(rng, 6), axis_at), (parts,), jnp.float32, least / len(shards), high / len(shards))
        gain = gain * jnp.repeat(jnp.exp(heights), dims[axis_at] // parts).reshape((-1,) + (1,) * (len(dims) - 1 - axis_at))
    return gain


def bell_draw(key, extent, width, reach, cuts=(), kind=jnp.bfloat16):
    drawn = jax.random.normal(key, extent, jnp.float32) * width
    if len(cuts) > 0:
        drawn = shard_levels(key, extent, cuts, -0.22, 0.18) * drawn
    return jnp.clip(drawn, min=-reach, max=reach).astype(kind)


def setup_inputs(seed: int = 0) -> dict:
    splits = jax.random.split(jax.random.key(seed), 19)
    hidden_in = bell_draw(splits[0], (MICRO, PACKS, SEQ, D), 1.0, 6.0, ((1, 8), (2, 4)))
    segment_ids = draw_segment_ids(jax.random.fold_in(splits[18], 71), 0)
    out_grad = bell_draw(splits[2], (MICRO, PACKS, SEQ, D), 1.0, 6.0, ((1, 8), (2, 4)))
    norm_gain = jnp.clip(1.0 + 0.18 * jax.random.normal(splits[3], (D,), jnp.float32), 0.099609375, 1.8984375).astype(jnp.bfloat16)
    w_qkv = bell_draw(splits[4], (D, QW + 2 * KW), D ** -0.5, 0.1875, ((0, 8),))
    w_o = bell_draw(splits[5], (QW, D), (HD // 2) ** -0.5, 1.0, ((0, 8),))
    w_zx = bell_draw(splits[6], (D, 2 * DI), D ** -0.5, 0.1875, ((0, 8),))
    w_bc = bell_draw(splits[7], (D, 2 * NS), D ** -0.5, 0.1875, ((0, 8),))
    w_dt = bell_draw(splits[8], (D, MH), D ** -0.5, 0.1875, ((0, 8),))
    conv_w = bell_draw(splits[9], (CONV, XC), CONV ** -0.5, 3.0, ((1, 8),))
    conv_b = bell_draw(splits[10], (XC,), 0.5, 3.0, ((0, 8),))
    dt_bias = jnp.clip(jax.random.uniform(splits[11], (MH,), jnp.float32, -6.5, -4.5), -6.5, -4.5)
    a_log = draw_a_log(jax.random.fold_in(splits[18], 71), 0)
    d_skip = jnp.clip(jax.random.uniform(splits[13], (MH,), jnp.float32, 0.5, 1.5), 0.5, 1.5)
    w_out = bell_draw(splits[14], (DI, D), DI ** -0.5, 0.15625, ((0, 8),))
    second_gain = jnp.clip(1.0 + 0.18 * jax.random.normal(splits[15], (D,), jnp.float32), 0.099609375, 1.8984375).astype(jnp.bfloat16)
    w_gate_up = bell_draw(splits[16], (D, 2 * FF), D ** -0.5, 0.1875, ((0, 8),))
    w_down = bell_draw(splits[17], (FF, D), (FF // 2) ** -0.5, 0.1875, ((0, 8),))
    return dict(hidden_in=hidden_in, segment_ids=segment_ids, out_grad=out_grad, norm_gain=norm_gain, w_qkv=w_qkv, w_o=w_o, w_zx=w_zx, w_bc=w_bc, w_dt=w_dt, conv_w=conv_w, conv_b=conv_b, dt_bias=dt_bias, a_log=a_log, d_skip=d_skip, w_out=w_out, second_gain=second_gain, w_gate_up=w_gate_up, w_down=w_down)


@jax.custom_vjp
def low(v):
    return lax.optimization_barrier(v.astype(jnp.bfloat16)).astype(jnp.float32)

@jax.custom_vjp
def low_back(v):
    return v

def low_keep(v):
    return (low(v), None)

def low_pass(kept, grad):
    return (grad,)

def back_keep(v):
    return (v, None)

def back_low(kept, grad):
    return (low(grad),)
low.defvjp(low_keep, low_pass)
low_back.defvjp(back_keep, back_low)
epsilon = 1e-05
rope_base = 100000000000.0
block_tokens = 64
highest = lax.Precision.HIGHEST

def matmul_high(left, right):
    return jnp.dot(left, right, precision=highest, preferred_element_type=jnp.float32)

def rotary_tables(positions):
    half_width = HD // 2
    exponents = jnp.arange(half_width, dtype=jnp.float32) * (2.0 / HD)
    inverse = jnp.exp(-exponents * math.log(rope_base))
    angles = positions[:, None] * inverse[None, :]
    cosine = jnp.concatenate([jnp.cos(angles), jnp.cos(angles)], axis=1)
    sine_table = jnp.concatenate([jnp.sin(angles), jnp.sin(angles)], axis=1)
    return (cosine, sine_table)

def rotate(values, cosine, sine_table):
    half_width = values.shape[-1] // 2
    first_half = values[..., :half_width]
    second_half = values[..., half_width:]
    turned = jnp.concatenate([-second_half, first_half], axis=-1)
    return values * cosine[:, None, :] + turned * sine_table[:, None, :]

def conv_mix(conv_ext, seg_ext, segments, conv_w, conv_b):
    length = segments.shape[0]
    summed = conv_b[None, :]
    for tap in range(CONV):
        same = (seg_ext[tap:tap + length] == segments)[:, None]
        summed = summed + jnp.where(same, conv_ext[tap:tap + length] * conv_w[tap][None, :], 0.0)
    return jax.nn.silu(summed)

def ssd_local(x_heads, step_size, decay_log, input_map, output_map, segments, prev_seg):
    length = segments.shape[0]
    cumulative = jnp.cumsum(decay_log, axis=0)
    order = jnp.arange(length)
    valid = ((order[:, None] >= order[None, :]) & (segments[:, None] == segments[None, :]))[:, :, None]
    spread = cumulative[:, None, :] - cumulative[None, :, :]
    kernel = jnp.where(valid, jnp.exp(jnp.where(valid, spread, 0.0)), 0.0)
    intersection = jnp.dot(output_map, input_map.T, precision=highest, preferred_element_type=jnp.float32)
    weighted = kernel * intersection[:, :, None]
    driven = x_heads * step_size[:, :, None]
    local_term = jnp.einsum('tsh,shp->thp', weighted, driven, precision=highest)
    carry_in = jnp.where((segments == prev_seg)[:, None], jnp.exp(cumulative), 0.0)
    tail_weight = jnp.where((segments == segments[-1])[:, None], jnp.exp(cumulative[-1][None, :] - cumulative), 0.0)
    decay_total = jnp.where(segments[-1] == prev_seg, jnp.exp(cumulative[-1]), 0.0)
    state_local = jnp.einsum('shp,sn->hpn', driven * tail_weight[:, :, None], input_map, precision=highest)
    return (local_term, carry_in, decay_total, state_local)

def from_carry(output_map, carry_in, state_in):
    return jnp.einsum('tn,hpn->thp', output_map, state_in, precision=highest) * carry_in[:, :, None]

def layer(segments, hidden, norm_gain, w_qkv, w_o, w_zx, w_bc, w_dt, conv_w, conv_b, dt_bias, a_log, d_skip, w_out, second_gain, w_gate_up, w_down):
    length = hidden.shape[0]
    inv_rms = lax.rsqrt(lax.optimization_barrier(jnp.mean(hidden * hidden, axis=-1, keepdims=True)) + epsilon)
    normed = low(hidden * inv_rms * norm_gain[None, :])
    projected = low_back(matmul_high(normed, w_qkv))
    positions = jnp.arange(length).astype(jnp.float32)
    cosine, sine_table = rotary_tables(positions)
    queries = low(rotate(projected[:, :QW].reshape(length, HEADS, HD), cosine, sine_table))
    key_rows = low(rotate(projected[:, QW:QW + KW].reshape(length, KV, HD), cosine, sine_table))
    value_rows = low(projected[:, QW + KW:].reshape(length, KV, HD))
    grouped = queries.reshape(length, KV, HEADS // KV, HD)
    scores = low_back(jnp.einsum('qvgd,kvd->vgqk', grouped, key_rows, precision=highest) / math.sqrt(HD))
    order = jnp.arange(length)
    allowed = (order[None, :] <= order[:, None]) & (segments[None, :] == segments[:, None])
    scores = jnp.where(allowed[None, None], scores, -1e+30)
    row_peak = lax.optimization_barrier(jnp.max(scores, axis=-1, keepdims=True))
    expo = jnp.exp(scores - row_peak)
    probability = expo / lax.optimization_barrier(jnp.sum(expo, axis=-1, keepdims=True))
    attended = jnp.einsum('vgqk,kvd->qvgd', low(probability), value_rows, precision=highest)
    attended = low(low_back(attended.reshape(length, QW)))
    attn_out = matmul_high(attended, w_o)
    inner_proj = low_back(matmul_high(normed, w_zx))
    mixed_bc = low_back(matmul_high(normed, w_bc))
    step_raw = low_back(matmul_high(normed, w_dt))
    gate_z = inner_proj[:, :DI]
    conv_in = low(jnp.concatenate([inner_proj[:, DI:], mixed_bc], axis=1))
    conv_ext = jnp.concatenate([jnp.zeros((CONV - 1, XC), jnp.float32), conv_in], axis=0)
    seg_ext = jnp.concatenate([jnp.full((CONV - 1,), -1, jnp.int32), segments.astype(jnp.int32)], axis=0)
    activated = conv_mix(conv_ext, seg_ext, segments, conv_w, conv_b)
    x_heads = activated[:, :DI].reshape(length, MH, MP)
    input_map = activated[:, DI:DI + NS]
    output_map = activated[:, DI + NS:]
    step_size = jax.nn.softplus(step_raw + dt_bias[None, :])
    decay_log = -step_size * jnp.exp(a_log)[None, :]
    blocks = length // block_tokens
    previous = jnp.concatenate([jnp.full((1,), -1, jnp.int32), segments[:-1].astype(jnp.int32)], axis=0)
    previous = previous.reshape(blocks, block_tokens)[:, 0]

    def advance(state_in, pieces):
        x_block, step_block, decay_block, in_block, out_block, seg_block, prev_block = pieces
        local_term, carry_in, decay_total, state_local = ssd_local(x_block, step_block, decay_block, in_block, out_block, seg_block, prev_block)
        outputs = local_term + from_carry(out_block, carry_in, state_in)
        return (decay_total[:, None, None] * state_in + state_local, outputs)
    _, outputs = lax.scan(jax.checkpoint(advance), jnp.zeros((MH, MP, NS), jnp.float32), (x_heads.reshape(blocks, block_tokens, MH, MP), step_size.reshape(blocks, block_tokens, MH), decay_log.reshape(blocks, block_tokens, MH), input_map.reshape(blocks, block_tokens, NS), output_map.reshape(blocks, block_tokens, NS), segments.reshape(blocks, block_tokens), previous))
    y_heads = outputs.reshape(length, MH, MP) + d_skip[None, :, None] * x_heads
    gated = low(low_back(y_heads.reshape(length, DI) * jax.nn.silu(gate_z)))
    mamba_out = matmul_high(gated, w_out)
    middle = low_back(hidden + attn_out + mamba_out)
    second_rms = lax.rsqrt(lax.optimization_barrier(jnp.mean(middle * middle, axis=-1, keepdims=True)) + epsilon)
    second_normed = low(middle * second_rms * second_gain[None, :])
    gate_up = low_back(matmul_high(second_normed, w_gate_up))
    hidden_units = low(low_back(jax.nn.silu(gate_up[:, :FF]) * gate_up[:, FF:]))
    return middle + matmul_high(hidden_units, w_down)

def reference(hidden_in, segment_ids, out_grad, norm_gain, w_qkv, w_o, w_zx, w_bc, w_dt, conv_w, conv_b, dt_bias, a_log, d_skip, w_out, second_gain, w_gate_up, w_down):
    params = tuple((weight.astype(jnp.float32) for weight in (norm_gain, w_qkv, w_o, w_zx, w_bc, w_dt, conv_w, conv_b, dt_bias, a_log, d_skip, w_out, second_gain, w_gate_up, w_down)))
    pack_count = MICRO * PACKS
    hidden_all = hidden_in.reshape(pack_count, SEQ, D)
    segments_all = segment_ids.reshape(pack_count, SEQ)
    grads_all = out_grad.reshape(pack_count, SEQ, D)

    def one_pack(totals, pack_items):
        hidden, segments, cotangent = pack_items
        forward = partial(layer, segments)
        result, pullback = jax.vjp(forward, hidden.astype(jnp.float32), *params)
        grads = pullback(cotangent.astype(jnp.float32))
        totals = tuple((total + grad for total, grad in zip(totals, grads[1:])))
        return (totals, (result.astype(jnp.bfloat16), grads[0].astype(jnp.bfloat16)))
    start = tuple((jnp.zeros_like(weight) for weight in params))
    totals, (results, input_grads) = lax.scan(one_pack, start, (hidden_all, segments_all, grads_all))
    return (results.reshape(MICRO, PACKS, SEQ, D), input_grads.reshape(MICRO, PACKS, SEQ, D), totals[0], totals[1], totals[2], totals[3], totals[4], totals[5], totals[6], totals[7], totals[8], totals[9], totals[10], totals[11], totals[12], totals[13], totals[14])
```

```python
import math

import jax
import jax.numpy as jnp
from jax import lax
from jax.sharding import PartitionSpec as P

HEADS = 8
KV = 2
HD = 64
MH = 24
MP = 64
NS = 128
CONV = 4
FF = 2048
QW = 512
KW = 128
DI = 1536
XC = 1792

epsilon = 1e-05
rope_base = 100000000000.0
f32 = jnp.float32
bf16 = jnp.bfloat16


def dot_plain(left, right):
    return jnp.dot(left, right, preferred_element_type=f32)


def dot_first(left, right):
    return lax.dot_general(left, right, (((0,), (0,)), ((), ())), preferred_element_type=f32)


def dot_last(left, right):
    return lax.dot_general(left, right, (((1,), (1,)), ((), ())), preferred_element_type=f32)


def swap(block, axis, bit):
    devices = range(lax.axis_size(axis))
    return lax.ppermute(block, axis, [(i, i ^ bit) for i in devices])


def ctx_gather(block):
    size = lax.axis_size("ctx")
    place = lax.axis_index("ctx")
    out = block[None]
    bit = size // 2
    while bit:
        other = swap(out, "ctx", bit)
        low = (place // bit) % 2 == 0
        out = jnp.where(low, jnp.stack([out, other], 1), jnp.stack([other, out], 1))
        out = out.reshape((-1,) + block.shape)
        bit //= 2
    return out


def ctx_scatter(parts):
    size = lax.axis_size("ctx")
    place = lax.axis_index("ctx")
    bit = 1
    while bit < size:
        mine = (place // bit) % 2
        parts = parts.reshape((-1, 2) + parts.shape[1:])
        keep = lax.dynamic_index_in_dim(parts, mine, 1, False)
        send = lax.dynamic_index_in_dim(parts, 1 - mine, 1, False)
        got = swap(send.astype(bf16), "ctx", bit)
        parts = keep.astype(f32) + got.astype(f32)
        bit *= 2
    return parts[0]


def everywhere_sum(value):
    for axis in ("ctx", "fsdp"):
        bit = 1
        while bit < lax.axis_size(axis):
            value = value + swap(value, axis, bit)
            bit *= 2
    return value


def to_owner_columns(rows, back):
    F, C = lax.axis_size("fsdp"), lax.axis_size("ctx")
    route = []
    for f in range(F):
        for c in range(C):
            pair = (f * C + c, ((f % (F // C)) * C + c) * C + f // (F // C))
            route.append(pair[::-1] if back else pair)
    return lax.ppermute(rows, ("fsdp", "ctx"), route)


def rotary_tables(positions):
    half_width = HD // 2
    exponents = jnp.arange(half_width, dtype=f32) * (2.0 / HD)
    inverse = jnp.exp(-exponents * math.log(rope_base))
    angles = positions[:, None] * inverse[None, :]
    cosine = jnp.concatenate([jnp.cos(angles), jnp.cos(angles)], axis=1)
    sine = jnp.concatenate([jnp.sin(angles), jnp.sin(angles)], axis=1)
    return (cosine, sine)


def rotate(values, cosine, sine):
    half = HD // 2
    turned = jnp.concatenate([-values[..., half:], values[..., :half]], axis=-1)
    return values * cosine[:, None, :] + turned * sine[:, None, :]


def unrotate(grads, cosine, sine):
    half = HD // 2
    scaled = grads * sine[:, None, :]
    turned = jnp.concatenate([scaled[..., half:], -scaled[..., :half]], axis=-1)
    return grads * cosine[:, None, :] + turned


def shifted(rows, distance):
    if distance == 0:
        return rows
    if distance > 0:
        return jnp.pad(rows, ((0, 0), (distance, 0), (0, 0)))[:, : rows.shape[1]]
    return jnp.pad(rows, ((0, 0), (0, -distance), (0, 0)))[:, -distance:]


def conv_masks(segments):
    masks = []
    for distance in range(CONV):
        behind = jnp.pad(segments, ((0, 0), (distance, 0)), constant_values=-1)
        masks.append((behind[:, : segments.shape[1]] == segments)[:, :, None])
    return masks


def mamba_forward(conv_in, dt_raw, gate_z, taps, bias, dt_bias, a_rate, skip, segments):
    micro, length, _ = conv_in.shape
    heads = dt_bias.shape[0]
    width = heads * MP
    masks = conv_masks(segments)
    conv_f = conv_in.astype(f32)
    behind = [jnp.where(masks[k], shifted(conv_f, k), 0.0) for k in range(CONV)]
    pre = bias[None, None, :]
    for k in range(CONV):
        pre = pre + behind[k] * taps[CONV - 1 - k][None, None, :]
    act = jax.nn.silu(pre)
    x_heads = act[..., :width].reshape(micro, length, heads, MP)
    b_map = act[..., width : width + NS].astype(bf16)
    c_map = act[..., width + NS :].astype(bf16)
    step_pre = dt_raw + dt_bias
    step = jax.nn.softplus(step_pre)
    decay_log = -step * a_rate
    cum = jnp.cumsum(decay_log, axis=1)
    order = jnp.arange(length)
    valid = (order[:, None] >= order[None, :])[None] & (
        segments[:, :, None] == segments[:, None, :]
    )
    cum_h = cum.transpose(0, 2, 1)
    spread = cum_h[:, :, :, None] - cum_h[:, :, None, :]
    kernel = jnp.exp(jnp.where(valid[:, None], spread, -1e30))
    cross = jnp.einsum("mtn,msn->mts", c_map, b_map, preferred_element_type=f32)
    weighted = kernel * cross[:, None]
    driven = x_heads * step[..., None]
    y_state = jnp.einsum(
        "mhts,mshp->mthp", weighted.astype(bf16), driven.astype(bf16), preferred_element_type=f32
    )
    y = (y_state + skip[:, None] * x_heads).reshape(micro, length, width)
    gated = (y * jax.nn.silu(gate_z)).astype(bf16)
    saved = (behind, pre, x_heads, b_map, c_map, step_pre, step, decay_log, kernel, cross, driven, y, masks)
    return gated, saved


def silu_slope(v):
    s = jax.nn.sigmoid(v)
    return s * (1.0 + v * (1.0 - s))


def mamba_backward(saved, d_gated, gate_z, taps, a_rate, skip):
    behind, pre, x_heads, b_map, c_map, step_pre, step, decay_log, kernel, cross, driven, y, masks = saved
    micro, length, heads, _ = x_heads.shape
    d_y = (d_gated * jax.nn.silu(gate_z)).reshape(micro, length, heads, MP)
    d_gate = d_gated * y * silu_slope(gate_z)
    d_y16 = d_y.astype(bf16)
    weighted = kernel * cross[:, None]
    d_weighted = jnp.einsum("mthp,mshp->mhts", d_y16, driven.astype(bf16), preferred_element_type=f32)
    d_driven = jnp.einsum("mhts,mthp->mshp", weighted.astype(bf16), d_y16, preferred_element_type=f32)
    d_cross = jnp.sum(d_weighted * kernel, axis=1).astype(bf16)
    pairs = d_weighted * weighted
    d_cum = (jnp.sum(pairs, axis=3) - jnp.sum(pairs, axis=2)).transpose(0, 2, 1)
    d_decay_log = jnp.cumsum(d_cum[:, ::-1], axis=1)[:, ::-1]
    d_c = jnp.einsum("mts,msn->mtn", d_cross, b_map, preferred_element_type=f32)
    d_b = jnp.einsum("mts,mtn->msn", d_cross, c_map, preferred_element_type=f32)
    d_x = d_driven * step[..., None] + skip[:, None] * d_y
    d_step = jnp.sum(d_driven * x_heads, axis=-1) - d_decay_log * a_rate
    d_dt = d_step * jax.nn.sigmoid(step_pre)
    g_dt_bias = jnp.sum(d_dt, axis=(0, 1))
    g_a_log = jnp.sum(d_decay_log * decay_log, axis=(0, 1))
    g_skip = jnp.sum(d_y * x_heads, axis=(0, 1, 3))
    d_act = jnp.concatenate([d_x.reshape(micro, length, heads * MP), d_b, d_c], axis=2)
    d_pre = d_act * silu_slope(pre)
    g_bias = jnp.sum(d_pre, axis=(0, 1))
    g_taps = jnp.stack([jnp.sum(d_pre * behind[CONV - 1 - j], axis=(0, 1)) for j in range(CONV)])
    d_conv = 0.0
    for k in range(CONV):
        d_conv = d_conv + shifted(jnp.where(masks[k], d_pre, 0.0), -k) * taps[CONV - 1 - k]
    return d_gate, d_conv, d_dt, g_taps, g_bias, g_dt_bias, g_a_log, g_skip


def attend(queries, keys, values, allowed, scale):
    scores = jnp.einsum("mqhd,mkd->mhqk", queries, keys, preferred_element_type=f32) * scale
    scores = jnp.where(allowed[:, None], scores, -1e30)
    peak = jnp.max(scores, axis=-1, keepdims=True)
    expo = jnp.exp(scores - peak)
    probability = expo / jnp.sum(expo, axis=-1, keepdims=True)
    attended = jnp.einsum(
        "mhqk,mkd->mqhd", probability.astype(bf16), values, preferred_element_type=f32
    )
    return probability, attended


def attend_back(probability, d_att, queries, keys, values, scale):
    d_prob = jnp.einsum("mqhd,mkd->mhqk", d_att, values, preferred_element_type=f32)
    delta = jnp.sum(probability * d_prob, axis=-1, keepdims=True)
    d_scores = (probability * (d_prob - delta)).astype(bf16)
    d_q = jnp.einsum("mhqk,mkd->mqhd", d_scores, keys, preferred_element_type=f32) * scale
    d_k = jnp.einsum("mhqk,mqhd->mkd", d_scores, queries, preferred_element_type=f32) * scale
    d_v = jnp.einsum(
        "mhqk,mqhd->mkd", probability.astype(bf16), d_att, preferred_element_type=f32
    )
    return d_q, d_k, d_v


def per_device(
    hidden_in,
    segment_ids,
    out_grad,
    norm_gain,
    w_qkv,
    w_o,
    w_zx,
    w_bc,
    w_dt,
    conv_w,
    conv_b,
    dt_bias,
    a_log,
    d_skip,
    w_out,
    second_gain,
    w_gate_up,
    w_down,
):
    micro, _, tokens, D = hidden_in.shape
    F, C = lax.axis_size("fsdp"), lax.axis_size("ctx")
    c = lax.axis_index("ctx")
    f = lax.axis_index("fsdp")
    length = tokens * C
    rows = micro * length
    qh, mh = HEADS // C, MH // C
    qw, dw, fw = QW // C, DI // C, FF // C
    kv = c * KV // C
    scale = 1.0 / math.sqrt(HD)
    dt_pad = 128 - mh

    def cols(weight, start, size):
        return lax.dynamic_slice_in_dim(weight, start, size, 1)

    block = w_qkv.shape[0]
    first_shard = jnp.concatenate(
        [
            cols(w_qkv, c * qw, qw),
            cols(w_qkv, QW + kv * HD, HD),
            cols(w_qkv, QW + KW + kv * HD, HD),
            cols(w_zx, c * dw, dw),
            cols(w_zx, DI + c * dw, dw),
            w_bc,
            cols(w_dt, c * mh, mh),
            jnp.zeros((block, dt_pad), bf16),
        ],
        axis=1,
    )
    gu_shard = jnp.concatenate([cols(w_gate_up, c * fw, fw), cols(w_gate_up, FF + c * fw, fw)], 1)
    ro, rz, rd = w_o.shape[0] // C, w_out.shape[0] // C, w_down.shape[0] // C
    row_shard = jnp.concatenate(
        [
            lax.dynamic_slice_in_dim(w_o, c * ro, ro, 0),
            lax.dynamic_slice_in_dim(w_out, c * rz, rz, 0),
            lax.dynamic_slice_in_dim(w_down, c * rd, rd, 0),
        ],
        axis=0,
    )
    row_shard = to_owner_columns(row_shard, False)
    xb = conv_b.shape[0]
    small_shard = jnp.concatenate(
        [conv_w.reshape(-1), conv_b, norm_gain, second_gain], axis=0
    )
    small_all = lax.all_gather(small_shard, "fsdp", axis=0, tiled=False)
    w_first = lax.all_gather(first_shard, "fsdp", axis=0, tiled=True)
    row_all = lax.all_gather(row_shard, "fsdp", axis=0, tiled=False)
    w_gu = lax.all_gather(gu_shard, "fsdp", axis=0, tiled=True)

    conv_all = small_all[:, : (CONV + 1) * xb].reshape(F, CONV + 1, xb)
    conv_all = conv_all.transpose(1, 0, 2).reshape(CONV + 1, XC).astype(f32)
    conv_own = jnp.concatenate([cols(conv_all, c * dw, dw), conv_all[:, DI:]], axis=1)
    taps, conv_bias = conv_own[:CONV], conv_own[CONV]
    gains = small_all[:, (CONV + 1) * xb :].astype(f32)
    gain = gains[:, :block].reshape(1, D)
    gain_two = gains[:, block:].reshape(1, D)
    w_o_own = row_all[:, :ro].reshape(F * ro, D)
    w_out_own = row_all[:, ro : ro + rz].reshape(F * rz, D)
    w_down_own = row_all[:, ro + rz :].reshape(F * rd, D)
    dtb = lax.dynamic_slice_in_dim(dt_bias, c * mh, mh, 0)
    a_rate = jnp.exp(lax.dynamic_slice_in_dim(a_log, c * mh, mh, 0))
    skip = lax.dynamic_slice_in_dim(d_skip, c * mh, mh, 0)

    def gather_tokens(own):
        return ctx_gather(own).transpose(1, 0, 2, 3).reshape(rows, D)

    def scatter_tokens(partial):
        return ctx_scatter(partial.reshape(micro, C, tokens, D).transpose(1, 0, 2, 3))

    hidden_own = hidden_in[:, 0].astype(f32)
    hidden = gather_tokens(hidden_in[:, 0]).astype(f32)
    cot = gather_tokens(out_grad[:, 0])
    segments = segment_ids[:, 0]
    order = jnp.arange(length)
    cosine, sine = rotary_tables(order.astype(f32))
    allowed = (order[None, :] <= order[:, None])[None] & (
        segments[:, None, :] == segments[:, :, None]
    )

    inv_rms = lax.rsqrt(jnp.mean(hidden * hidden, axis=-1, keepdims=True) + epsilon)
    normed = (hidden * inv_rms * gain).astype(bf16)
    first = dot_plain(normed, w_first).reshape(micro, length, -1)
    at = qw
    queries = rotate(first[..., :qw].reshape(micro, length, qh, HD), cosine, sine).astype(bf16)
    keys = rotate(first[..., at : at + HD].reshape(micro, length, 1, HD), cosine, sine)[:, :, 0].astype(bf16)
    values = first[..., at + HD : at + 2 * HD].astype(bf16)
    at += 2 * HD
    gate_z = first[..., at : at + dw]
    at += dw
    conv_in = first[..., at : at + dw + 2 * NS].astype(bf16)
    at += dw + 2 * NS
    dt_raw = first[..., at : at + mh]

    probability, attended = attend(queries, keys, values, allowed, scale)
    attended = attended.reshape(rows, qw).astype(bf16)
    gated, saved = mamba_forward(conv_in, dt_raw, gate_z, taps, conv_bias, dtb, a_rate, skip, segments)
    gated = gated.reshape(rows, dw)
    mixed = dot_plain(attended, w_o_own) + dot_plain(gated, w_out_own)
    middle = hidden_own + scatter_tokens(mixed)
    second_rms = lax.rsqrt(jnp.mean(middle * middle, axis=-1, keepdims=True) + epsilon)
    second_normed = gather_tokens((middle * second_rms * gain_two).astype(bf16))

    gate_up = dot_plain(second_normed, w_gu)
    gate_part, up_part = gate_up[:, :fw], gate_up[:, fw:]
    sig = jax.nn.sigmoid(gate_part)
    gate_silu = gate_part * sig
    units = (gate_silu * up_part).astype(bf16)
    d_units = dot_last(cot, w_down_own).astype(bf16).astype(f32)
    d_gate_up = jnp.concatenate(
        [d_units * up_part * (sig * (1.0 + gate_part * (1.0 - sig))), d_units * gate_silu], axis=1
    ).astype(bf16)
    d_second = scatter_tokens(dot_last(d_gate_up, w_gu))
    block_out = (middle + scatter_tokens(dot_plain(units, w_down_own))).astype(bf16)
    g_gu = dot_first(second_normed, d_gate_up)
    g_down = dot_first(units, cot)

    g_gain_two = jnp.sum(d_second * middle * second_rms, axis=(0, 1))
    scaled_two = d_second * gain_two
    d_middle_own = (
        out_grad[:, 0].astype(f32)
        + second_rms * scaled_two
        - middle * second_rms**3 * jnp.mean(middle * scaled_two, axis=-1, keepdims=True)
    ).astype(bf16)
    d_middle = gather_tokens(d_middle_own)
    d_gated = dot_last(d_middle, w_out_own).astype(bf16).astype(f32).reshape(micro, length, dw)
    d_att = dot_last(d_middle, w_o_own).astype(bf16).reshape(micro, length, qh, HD)
    g_o = dot_first(attended, d_middle)
    g_out = dot_first(gated, d_middle)

    d_q, d_k, d_v = attend_back(probability, d_att, queries, keys, values, scale)
    d_q = unrotate(d_q, cosine, sine).reshape(micro, length, qw)
    d_k = unrotate(d_k[:, :, None], cosine, sine)[:, :, 0]
    d_gate, d_conv, d_dt, g_taps, g_bias, g_dtb, g_alog, g_skip = mamba_backward(
        saved, d_gated, gate_z, taps, a_rate, skip
    )
    d_first = jnp.concatenate(
        [d_q, d_k, d_v, d_gate, d_conv, d_dt, jnp.zeros((micro, length, dt_pad), f32)], axis=2
    )
    d_first = d_first.astype(bf16).reshape(rows, -1)
    d_normed_part = dot_last(d_first, w_first)
    g_first = dot_first(normed, d_first)
    g_gain = jnp.sum(d_normed_part * hidden * inv_rms, axis=0)
    d_normed = scatter_tokens(d_normed_part)
    inv_own = lax.rsqrt(jnp.mean(hidden_own * hidden_own, axis=-1, keepdims=True) + epsilon)
    scaled = d_normed * gain
    grad_in = (
        d_middle_own.astype(f32)
        + inv_own * scaled
        - hidden_own * inv_own**3 * jnp.mean(hidden_own * scaled, axis=-1, keepdims=True)
    ).astype(bf16)

    ffn = jnp.concatenate([g_gu.reshape(F, block, -1), g_down.reshape(F, rd, D)], axis=1)
    ffn = lax.psum_scatter(ffn.astype(bf16), "fsdp", scatter_dimension=0, tiled=False)
    mix = jnp.concatenate([g_o.reshape(F, ro, D), g_out.reshape(F, rz, D)], axis=1)
    mix = lax.psum_scatter(mix.astype(bf16), "fsdp", scatter_dimension=0, tiled=False)
    first_sum = lax.psum_scatter(g_first.astype(bf16), "fsdp", scatter_dimension=0, tiled=True)
    turned = to_owner_columns(jnp.concatenate([mix, ffn[block:]], axis=0), True)
    turned = ctx_gather(turned).astype(f32)
    grad_o = turned[:, :ro].reshape(C * ro, D)
    grad_out = turned[:, ro : ro + rz].reshape(C * rz, D)
    grad_down = turned[:, ro + rz :].reshape(C * rd, D)

    def side(parts):
        return jnp.concatenate([parts[i] for i in range(C)], axis=1)

    gu_all = ctx_gather(ffn[:block]).astype(f32)
    grad_gate_up = jnp.concatenate([side(gu_all[:, :, :fw]), side(gu_all[:, :, fw:])], axis=1)
    first_all = ctx_gather(first_sum).astype(f32)
    at = qw
    kv_pairs = first_all[:, :, at : at + 2 * HD].reshape(KV, C // KV, block, 2 * HD).sum(1)
    grad_qkv = jnp.concatenate(
        [side(first_all[:, :, :qw])]
        + [kv_pairs[j, :, :HD] for j in range(KV)]
        + [kv_pairs[j, :, HD:] for j in range(KV)],
        axis=1,
    )
    at += 2 * HD
    grad_zx = jnp.concatenate(
        [side(first_all[:, :, at : at + dw]), side(first_all[:, :, at + dw : at + 2 * dw])], axis=1
    )
    at += 2 * dw
    grad_bc = first_all[:, :, at : at + 2 * NS].sum(0)
    at += 2 * NS
    grad_dt = side(first_all[:, :, at : at + mh])

    g_conv = jnp.concatenate([g_taps, g_bias[None]], axis=0)
    conv_x = lax.dynamic_update_slice(
        jnp.zeros((CONV + 1, DI), f32), g_conv[:, :dw], (0, c * dw)
    )
    conv_full = jnp.concatenate([conv_x, g_conv[:, dw:]], axis=1)
    conv_full = conv_full.reshape(CONV + 1, F, xb).transpose(1, 0, 2).reshape(F, -1)
    small = jnp.concatenate([conv_full, g_gain.reshape(F, block), g_gain_two.reshape(F, block)], 1)
    heads = jnp.stack([g_dtb, g_alog, g_skip])
    heads = lax.dynamic_update_slice(jnp.zeros((3, MH), f32), heads, (0, c * mh))
    small = lax.psum_scatter(small, "fsdp", scatter_dimension=0, tiled=False)
    small = lax.psum(small, "ctx")
    heads = lax.psum(heads, ("fsdp", "ctx"))
    conv_sum = small[: (CONV + 1) * xb].reshape(CONV + 1, xb)
    at = (CONV + 1) * xb
    return (
        block_out[:, None],
        grad_in[:, None],
        small[at : at + block],
        grad_qkv,
        grad_o,
        grad_zx,
        grad_bc,
        grad_dt,
        conv_sum[:CONV],
        conv_sum[CONV],
        heads[0],
        heads[1],
        heads[2],
        grad_out,
        small[at + block :],
        grad_gate_up,
        grad_down,
    )


def solution(mesh):
    tokens = P(None, "fsdp", "ctx", None)
    rows = P("fsdp", None)
    return jax.shard_map(
        per_device,
        mesh=mesh,
        in_specs=(
            tokens,
            P(None, "fsdp", None),
            tokens,
            P("fsdp"),
            rows,
            rows,
            rows,
            rows,
            rows,
            P(None, "fsdp"),
            P("fsdp"),
            P(),
            P(),
            P(),
            rows,
            P("fsdp"),
            rows,
            rows,
        ),
        out_specs=(
            tokens,
            tokens,
            P("fsdp"),
            rows,
            rows,
            rows,
            rows,
            rows,
            P(None, "fsdp"),
            P("fsdp"),
            P(),
            P(),
            P(),
            rows,
            P("fsdp"),
            rows,
            rows,
        ),
        check_vma=False,
    )
```

```python
import math

import jax
import jax.numpy as jnp
from jax import lax
from jax.experimental import pallas as pl
from jax.experimental.pallas import tpu as pltpu
from jax.sharding import PartitionSpec as P

HEADS = 8
KV = 2
HD = 64
MH = 24
MP = 64
NS = 128
CONV = 4
FF = 2048
QW = 512
KW = 128
DI = 1536
XC = 1792

epsilon = 1e-05
rope_base = 100000000000.0
f32 = jnp.float32
bf16 = jnp.bfloat16


def dot_plain(left, right):
    return jnp.dot(left, right, preferred_element_type=f32)


def dot_first(left, right):
    return lax.dot_general(left, right, (((0,), (0,)), ((), ())), preferred_element_type=f32)


def dot_last(left, right):
    return lax.dot_general(left, right, (((1,), (1,)), ((), ())), preferred_element_type=f32)


def swap(block, axis, bit):
    devices = range(lax.axis_size(axis))
    return lax.ppermute(block, axis, [(i, i ^ bit) for i in devices])


def pair_gather(block, axis):
    size = lax.axis_size(axis)
    place = lax.axis_index(axis)
    out = block[None]
    bit = size // 2
    while bit:
        other = swap(out, axis, bit)
        low = (place // bit) % 2 == 0
        out = jnp.where(low, jnp.stack([out, other], 1), jnp.stack([other, out], 1))
        out = out.reshape((-1,) + block.shape)
        bit //= 2
    return out


def ctx_gather(block):
    return pair_gather(block, "ctx")


def line_groups():
    half = lax.axis_size("fsdp") // 2
    return [[2 * k + x for k in range(half)] for x in range(2)]


def line_gather(shard):
    return lax.all_gather(shard, "fsdp", axis=0, tiled=False, axis_index_groups=line_groups())


def join_pairs(column):
    first = lax.axis_index("fsdp") % 2 == 0
    other = swap(column, "fsdp", 1)
    both = jnp.where(first, jnp.stack([column, other], 1), jnp.stack([other, column], 1))
    return both.reshape((-1,) + column.shape[1:])


def fsdp_scatter(parts):
    column = lax.psum_scatter(
        parts.reshape((-1, 2) + parts.shape[1:]).astype(bf16),
        "fsdp",
        scatter_dimension=0,
        tiled=False,
        axis_index_groups=line_groups(),
    )
    mine = lax.axis_index("fsdp") % 2
    keep = lax.dynamic_index_in_dim(column, mine, 0, False)
    send = lax.dynamic_index_in_dim(column, 1 - mine, 0, False)
    return keep.astype(f32) + swap(send, "fsdp", 1).astype(f32)


def ctx_scatter(parts):
    size = lax.axis_size("ctx")
    place = lax.axis_index("ctx")
    bit = 1
    while bit < size:
        mine = (place // bit) % 2
        parts = parts.reshape((-1, 2) + parts.shape[1:])
        keep = lax.dynamic_index_in_dim(parts, mine, 1, False)
        send = lax.dynamic_index_in_dim(parts, 1 - mine, 1, False)
        got = swap(send.astype(bf16), "ctx", bit)
        parts = keep.astype(f32) + got.astype(f32)
        bit *= 2
    return parts[0]


def everywhere_sum(value):
    for axis in ("ctx", "fsdp"):
        bit = 1
        while bit < lax.axis_size(axis):
            value = value + swap(value, axis, bit)
            bit *= 2
    return value


def to_owner_columns(rows, back):
    F, C = lax.axis_size("fsdp"), lax.axis_size("ctx")
    route = []
    for f in range(F):
        for c in range(C):
            pair = (f * C + c, ((f % (F // C)) * C + c) * C + f // (F // C))
            route.append(pair[::-1] if back else pair)
    return lax.ppermute(rows, ("fsdp", "ctx"), route)


def rotary_tables(positions):
    half_width = HD // 2
    exponents = jnp.arange(half_width, dtype=f32) * (2.0 / HD)
    inverse = jnp.exp(-exponents * math.log(rope_base))
    angles = positions[:, None] * inverse[None, :]
    cosine = jnp.concatenate([jnp.cos(angles), jnp.cos(angles)], axis=1)
    sine = jnp.concatenate([jnp.sin(angles), jnp.sin(angles)], axis=1)
    return (cosine, sine)


def mixer_tables(segments, conv_own, dt_bias, a_rate, skip):
    micro, length = segments.shape
    cosine, sine = rotary_tables(jnp.arange(length).astype(f32))
    columns = []
    for distance in range(CONV):
        behind = jnp.pad(segments, ((0, 0), (distance, 0)), constant_values=-1)[:, :length]
        columns.append((behind == segments).astype(f32))
    columns.append(segments.astype(f32))
    col = jnp.pad(jnp.stack(columns, axis=2), ((0, 0), (0, 0), (0, 128 - len(columns))))
    row = jnp.broadcast_to(segments.astype(f32)[:, None, :], (micro, 8, length))
    conv = jnp.pad(conv_own, ((0, 8 - conv_own.shape[0]), (0, 0)))
    heads = dt_bias.shape[0]
    head = jnp.pad(jnp.stack([dt_bias, a_rate]), ((0, 6), (0, 128 - heads)))
    skip = jnp.broadcast_to(skip[:, None], (heads, MP)).reshape(1, heads * MP)
    double = lambda table: jnp.concatenate([table, table], axis=1)
    return col, row, double(cosine), double(sine), conv, head, skip


def lane_index(shape):
    return lax.broadcasted_iota(jnp.int32, shape, 1)


def turn(tile, forward):
    up = pltpu.roll(tile, 128 - HD // 2, 1)
    down = pltpu.roll(tile, HD // 2, 1)
    low = lane_index(tile.shape) % HD < HD // 2
    return jnp.where(low, -up, down) if forward else jnp.where(low, up, -down)


def half_select(first, second):
    return jnp.where(lane_index(first.shape) < HD, first, second)


def half_only(tile, which):
    low = lane_index(tile.shape) < HD
    return jnp.where(low if which == 0 else jnp.logical_not(low), tile, jnp.zeros_like(tile))


def allowed_pairs(col, row):
    length = col.shape[0]
    order_t = lax.broadcasted_iota(jnp.int32, (length, length), 0)
    order_s = lax.broadcasted_iota(jnp.int32, (length, length), 1)
    return (order_s <= order_t) & (col[:, CONV : CONV + 1] == row[0:1, :])


def mixer_state(conv_f, dt_raw, col, conv, head):
    length = conv_f.shape[0]
    behind = [col[:, 0:1] * conv_f]
    for k in range(1, CONV):
        behind.append(col[:, k : k + 1] * pltpu.roll(conv_f, k, 0))
    pre = conv[CONV : CONV + 1, :]
    for k in range(CONV):
        pre = pre + behind[k] * conv[CONV - 1 - k : CONV - k, :]
    step_pre = dt_raw + head[0:1, :]
    step = jnp.maximum(step_pre, 0.0) + jnp.log1p(jnp.exp(-jnp.abs(step_pre)))
    decay_log = -step * head[1:2, :]
    order_t = lax.broadcasted_iota(jnp.int32, (length, length), 0)
    order_s = lax.broadcasted_iota(jnp.int32, (length, length), 1)
    lower = (order_s <= order_t).astype(f32)
    cum = jnp.dot(lower, decay_log, precision=lax.Precision.HIGHEST, preferred_element_type=f32)
    return behind, pre, step_pre, step, decay_log, cum


def decay_kernel(cum, cum_t, valid, h):
    return jnp.exp(jnp.where(valid, cum[:, h : h + 1] - cum_t[h : h + 1, :], -1e30))


def softmax_rows(queries, keys, valid, scale):
    scores = jnp.where(valid, dot_last(queries, keys) * scale, -1e30)
    peak = jnp.max(scores, axis=-1, keepdims=True)
    expo = jnp.exp(scores - peak)
    return expo / jnp.sum(expo, axis=-1, keepdims=True)


def forward_body(
    hidden_ref,
    gain_ref,
    w_ref,
    col_ref,
    row_ref,
    cos_ref,
    sin_ref,
    conv_ref,
    head_ref,
    skip_ref,
    normed_ref,
    qkv_ref,
    gate_ref,
    conv_in_ref,
    dt_ref,
    y_ref,
    mixed_ref,
):
    scale = 1.0 / math.sqrt(HD)
    dw = gate_ref.shape[1]
    heads = dw // MP
    hidden = hidden_ref[...].astype(f32)
    inv_rms = lax.rsqrt(jnp.mean(hidden * hidden, axis=-1, keepdims=True) + epsilon)
    normed = (hidden * inv_rms * gain_ref[...]).astype(bf16)
    normed_ref[...] = normed
    first = dot_plain(normed, w_ref[...])
    col, row = col_ref[0], row_ref[0]
    valid = allowed_pairs(col, row)
    cos, sin = cos_ref[...], sin_ref[...]
    q = first[:, :128]
    q = (q * cos + turn(q, True) * sin).astype(bf16)
    kv = first[:, 128:256]
    kv = half_select(kv * cos + turn(kv, True) * sin, kv)
    qkv_ref[:, :128] = q
    qkv_ref[:, 128:] = kv.astype(bf16)
    kv_turned = pltpu.roll(kv, HD, 1)
    keys = half_select(kv, kv_turned).astype(bf16)
    values = half_select(kv_turned, kv).astype(bf16)
    outs = []
    for h in range(2):
        probability = softmax_rows(half_only(q, h), keys, valid, scale)
        outs.append(dot_plain(probability.astype(bf16), values))
    mixed_ref[:, :128] = half_select(outs[0], outs[1]).astype(bf16)

    gate_z = first[:, 256 : 256 + dw]
    gate_ref[...] = gate_z
    conv_in = first[:, 256 + dw : 256 + 2 * dw + 2 * NS].astype(bf16)
    conv_in_ref[...] = conv_in
    dt_raw = first[:, 256 + 2 * dw + 2 * NS :]
    dt_ref[...] = dt_raw
    _, pre, _, step, _, cum = mixer_state(conv_in.astype(f32), dt_raw, col, conv_ref[...], head_ref[...])
    act = pre * jax.nn.sigmoid(pre)
    cum_t = jnp.transpose(cum)
    b_map = act[:, dw : dw + NS].astype(bf16)
    c_map = act[:, dw + NS :].astype(bf16)
    cross = dot_last(c_map, b_map)
    for j in range(heads // 2):
        x = act[:, 128 * j : 128 * (j + 1)]
        driven = (x * half_select_col(step, 2 * j, x.shape)).astype(bf16)
        pair = []
        for h in (2 * j, 2 * j + 1):
            weighted = decay_kernel(cum, cum_t, valid, h) * cross
            pair.append(dot_plain(weighted.astype(bf16), driven))
        y = half_select(pair[0], pair[1]) + skip_ref[:, 128 * j : 128 * (j + 1)] * x
        y_ref[:, 128 * j : 128 * (j + 1)] = y
        z = gate_z[:, 128 * j : 128 * (j + 1)]
        mixed_ref[:, 128 * (j + 1) : 128 * (j + 2)] = (y * z * jax.nn.sigmoid(z)).astype(bf16)


def half_select_col(columns, h, shape):
    return jnp.where(lane_index(shape) < MP, columns[:, h : h + 1], columns[:, h + 1 : h + 2])


def backward_body(
    d_mid_ref,
    hidden_ref,
    w_ref,
    w_mix_ref,
    col_ref,
    row_ref,
    cos_ref,
    sin_ref,
    conv_ref,
    head_ref,
    skip_ref,
    normed_ref,
    qkv_ref,
    gate_ref,
    conv_in_ref,
    dt_ref,
    y_ref,
    mixed_ref,
    d_normed_ref,
    g_first_ref,
    g_mix_ref,
    g_gain_ref,
    g_conv_ref,
    g_head_ref,
    g_skip_ref,
    acc_first,
    acc_mix,
    d_first,
):
    scale = 1.0 / math.sqrt(HD)
    dw = gate_ref.shape[1]
    heads = dw // MP
    at_conv = 256 + dw
    at_dt = at_conv + dw + 2 * NS
    first_step = pl.program_id(0) == 0

    @pl.when(first_step)
    def _():
        acc_first[...] = jnp.zeros_like(acc_first)
        acc_mix[...] = jnp.zeros_like(acc_mix)
        g_gain_ref[...] = jnp.zeros_like(g_gain_ref)
        g_conv_ref[...] = jnp.zeros_like(g_conv_ref)
        g_head_ref[...] = jnp.zeros_like(g_head_ref)
        g_skip_ref[...] = jnp.zeros_like(g_skip_ref)

    col, row = col_ref[0], row_ref[0]
    valid = allowed_pairs(col, row)
    length = col.shape[0]
    d_mid = d_mid_ref[...]
    acc_mix[...] += dot_first(mixed_ref[...], d_mid)
    d_mixed = dot_last(d_mid, w_mix_ref[...]).astype(bf16)

    cos, sin = cos_ref[...], sin_ref[...]
    q = qkv_ref[:, :128]
    kv = qkv_ref[:, 128:].astype(f32)
    kv_turned = pltpu.roll(kv, HD, 1)
    keys = half_select(kv, kv_turned).astype(bf16)
    values = half_select(kv_turned, kv).astype(bf16)
    d_att = d_mixed[:, :128]
    d_q, d_k, d_v = [], 0.0, 0.0
    for h in range(2):
        q_h = half_only(q, h)
        d_att_h = half_only(d_att, h)
        probability = softmax_rows(q_h, keys, valid, scale)
        d_prob = dot_last(d_att_h, values)
        delta = jnp.sum(probability * d_prob, axis=-1, keepdims=True)
        d_scores = (probability * (d_prob - delta)).astype(bf16)
        d_q.append(dot_plain(d_scores, keys))
        d_k = d_k + dot_first(d_scores, q_h)
        d_v = d_v + dot_first(probability.astype(bf16), d_att_h)
    d_q = half_select(d_q[0], d_q[1]) * scale
    d_k = (d_k + pltpu.roll(d_k, HD, 1)) * scale
    d_v = d_v + pltpu.roll(d_v, HD, 1)
    d_first[:, :128] = (d_q * cos + turn(d_q * sin, False)).astype(bf16)
    d_first[:, 128:256] = half_select(d_k * cos + turn(d_k * sin, False), d_v).astype(bf16)

    conv = conv_ref[...]
    behind, pre, step_pre, step, decay_log, cum = mixer_state(
        conv_in_ref[...].astype(f32), dt_ref[...], col, conv, head_ref[...]
    )
    sig = jax.nn.sigmoid(pre)
    act = pre * sig
    slope = sig * (1.0 + pre * (1.0 - sig))
    cum_t = jnp.transpose(cum)
    b_map = act[:, dw : dw + NS].astype(bf16)
    c_map = act[:, dw + NS :].astype(bf16)
    cross = dot_last(c_map, b_map)
    d_cross = jnp.zeros((length, length), f32)
    lanes = lane_index((length, 128))
    row_sums = jnp.zeros((length, 128), f32)
    x_sums = jnp.zeros((length, 128), f32)
    col_sums = []
    d_x_parts = []
    for j in range(heads // 2):
        part = slice(128 * j, 128 * (j + 1))
        z = gate_ref[:, part]
        z_sig = jax.nn.sigmoid(z)
        d_gated = d_mixed[:, 128 * (j + 1) : 128 * (j + 2)].astype(f32)
        d_first[:, 256 + 128 * j : 256 + 128 * (j + 1)] = (
            d_gated * y_ref[:, part] * (z_sig * (1.0 + z * (1.0 - z_sig)))
        ).astype(bf16)
        d_y = d_gated * (z * z_sig)
        d_y16 = d_y.astype(bf16)
        x = act[:, part]
        step_x = half_select_col(step, 2 * j, x.shape)
        driven = (x * step_x).astype(bf16)
        pair = []
        for h in (2 * j, 2 * j + 1):
            kernel = decay_kernel(cum, cum_t, valid, h)
            weighted = kernel * cross
            d_weighted = dot_last(half_only(d_y16, h - 2 * j), driven)
            d_cross = d_cross + d_weighted * kernel
            pairs = d_weighted * weighted
            row_sums = jnp.where(lanes == h, jnp.sum(pairs, axis=1, keepdims=True), row_sums)
            col_sums.append(jnp.sum(pairs, axis=0, keepdims=True))
            pair.append(dot_first(weighted.astype(bf16), d_y16))
        d_driven = half_select(pair[0], pair[1])
        d_x_parts.append(d_driven * step_x + skip_ref[:, part] * d_y)
        dx = d_driven * x
        for h in (2 * j, 2 * j + 1):
            x_sums = jnp.where(
                lanes == h, jnp.sum(half_only(dx, h - 2 * j), axis=1, keepdims=True), x_sums
            )
        g_skip_ref[:, part] += jnp.sum(d_y * x, axis=0, keepdims=True)
    col_sums = jnp.concatenate(col_sums + [jnp.zeros((128 - heads, length), f32)], axis=0)
    d_cum = row_sums - jnp.transpose(col_sums)
    order_t = lax.broadcasted_iota(jnp.int32, (length, length), 0)
    order_s = lax.broadcasted_iota(jnp.int32, (length, length), 1)
    upper = (order_s >= order_t).astype(f32)
    d_decay = jnp.dot(upper, d_cum, precision=lax.Precision.HIGHEST, preferred_element_type=f32)
    d_dt = (x_sums - d_decay * head_ref[1:2, :]) * jax.nn.sigmoid(step_pre)
    d_first[:, at_dt:] = d_dt.astype(bf16)
    g_head_ref[0:1, :] += jnp.sum(d_dt, axis=0, keepdims=True)
    g_head_ref[1:2, :] += jnp.sum(d_decay * decay_log, axis=0, keepdims=True)
    d_cross16 = d_cross.astype(bf16)
    d_act = d_x_parts + [dot_first(d_cross16, c_map), dot_plain(d_cross16, b_map)]
    for i, piece in enumerate(d_act):
        part = slice(128 * i, 128 * (i + 1))
        d_pre = piece * slope[:, part]
        g_conv_ref[CONV : CONV + 1, part] += jnp.sum(d_pre, axis=0, keepdims=True)
        d_conv = 0.0
        for k in range(CONV):
            tap = CONV - 1 - k
            g_conv_ref[tap : tap + 1, part] += jnp.sum(d_pre * behind[k][:, part], axis=0, keepdims=True)
            moved = col[:, k : k + 1] * d_pre
            if k:
                moved = pltpu.roll(moved, length - k, 0)
            d_conv = d_conv + moved * conv[tap : tap + 1, part]
        d_first[:, at_conv + 128 * i : at_conv + 128 * (i + 1)] = d_conv.astype(bf16)

    d_all = d_first[...]
    d_normed = dot_last(d_all, w_ref[...])
    d_normed_ref[...] = d_normed
    hidden = hidden_ref[...].astype(f32)
    inv_rms = lax.rsqrt(jnp.mean(hidden * hidden, axis=-1, keepdims=True) + epsilon)
    g_gain_ref[...] += jnp.sum(d_normed * (hidden * inv_rms), axis=0, keepdims=True)
    acc_first[...] += dot_first(normed_ref[...], d_all)

    @pl.when(pl.program_id(0) == pl.num_programs(0) - 1)
    def _():
        g_first_ref[...] = acc_first[...].astype(bf16)
        g_mix_ref[...] = acc_mix[...].astype(bf16)


def ffn_body(x_ref, cot_ref, gu_ref, down_ref, d_second_ref, out_ref, g_gu_ref, g_down_ref, acc_gu, acc_down):
    fw = down_ref.shape[0]

    @pl.when(pl.program_id(0) == 0)
    def _():
        acc_gu[...] = jnp.zeros_like(acc_gu)
        acc_down[...] = jnp.zeros_like(acc_down)

    x, cot = x_ref[...], cot_ref[...]
    gate_up = dot_plain(x, gu_ref[...])
    gate, up = gate_up[:, :fw], gate_up[:, fw:]
    sig = jax.nn.sigmoid(gate)
    gate_silu = gate * sig
    d_units = dot_last(cot, down_ref[...]).astype(bf16).astype(f32)
    d_gate = (d_units * up * (sig * (1.0 + gate * (1.0 - sig)))).astype(bf16)
    d_up = (d_units * gate_silu).astype(bf16)
    d_second_ref[...] = dot_last(d_gate, gu_ref[:, :fw]) + dot_last(d_up, gu_ref[:, fw:])
    units = (gate_silu * up).astype(bf16)
    out_ref[...] = dot_plain(units, down_ref[...])
    acc_gu[:, :fw] += dot_first(x, d_gate)
    acc_gu[:, fw:] += dot_first(x, d_up)
    acc_down[...] += dot_first(units, cot)

    @pl.when(pl.program_id(0) == pl.num_programs(0) - 1)
    def _():
        g_gu_ref[...] = acc_gu[...].astype(bf16)
        g_down_ref[...] = acc_down[...].astype(bf16)


def per_pack(block_rows, width):
    return pl.BlockSpec((block_rows, width), lambda m: (m, 0))


def per_pack3(rows, width):
    return pl.BlockSpec((1, rows, width), lambda m: (m, 0, 0))


def whole(shape):
    return pl.BlockSpec(shape, lambda m: (0,) * len(shape))


def struct(shape, kind):
    return jax.ShapeDtypeStruct(shape, kind)


params = pltpu.CompilerParams(
    dimension_semantics=("arbitrary",), vmem_limit_bytes=56 * 1024 * 1024
)


def mixer_forward(hidden, gain, w_first, tables, micro):
    rows, D = hidden.shape
    length = rows // micro
    col, row, cos, sin, conv, head, skip = tables
    dw, width = skip.shape[1], w_first.shape[1]
    cw = conv.shape[1]
    shapes = [(D, bf16), (256, bf16), (dw, f32), (cw, bf16), (128, f32), (dw, f32), (128 + dw, bf16)]
    return pl.pallas_call(
        forward_body,
        grid=(micro,),
        in_specs=[
            per_pack(length, D),
            whole(gain.shape),
            whole(w_first.shape),
            per_pack3(length, 128),
            per_pack3(8, length),
            whole(cos.shape),
            whole(sin.shape),
            whole(conv.shape),
            whole(head.shape),
            whole(skip.shape),
        ],
        out_specs=[per_pack(length, n) for n, _ in shapes],
        out_shape=[struct((rows, n), kind) for n, kind in shapes],
        compiler_params=params,
        name="mixer_forward",
    )(hidden, gain, w_first, col, row, cos, sin, conv, head, skip)


def mixer_backward(d_middle, hidden, w_first, w_mix, tables, saved, micro):
    rows, D = hidden.shape
    length = rows // micro
    col, row, cos, sin, conv, head, skip = tables
    width = w_first.shape[1]
    flat = [whole(a.shape) for a in (cos, sin, conv, head, skip)]
    sums = [w_first.shape, w_mix.shape, (1, D), conv.shape, head.shape, skip.shape]
    kinds = [bf16, bf16, f32, f32, f32, f32]
    return pl.pallas_call(
        backward_body,
        grid=(micro,),
        in_specs=[
            per_pack(length, D),
            per_pack(length, D),
            whole(w_first.shape),
            whole(w_mix.shape),
            per_pack3(length, 128),
            per_pack3(8, length),
        ]
        + flat
        + [per_pack(length, a.shape[1]) for a in saved],
        out_specs=[per_pack(length, D)] + [whole(s) for s in sums],
        out_shape=[struct((rows, D), f32)] + [struct(s, k) for s, k in zip(sums, kinds)],
        scratch_shapes=[
            pltpu.VMEM(w_first.shape, f32),
            pltpu.VMEM(w_mix.shape, f32),
            pltpu.VMEM((length, width), bf16),
        ],
        compiler_params=params,
        name="mixer_backward",
    )(d_middle, hidden, w_first, w_mix, col, row, cos, sin, conv, head, skip, *saved)


def ffn_both(x, cot, w_gu, w_down, micro):
    rows, D = x.shape
    length = rows // micro
    return pl.pallas_call(
        ffn_body,
        grid=(micro,),
        in_specs=[per_pack(length, D), per_pack(length, D), whole(w_gu.shape), whole(w_down.shape)],
        out_specs=[per_pack(length, D), per_pack(length, D), whole(w_gu.shape), whole(w_down.shape)],
        out_shape=[
            struct((rows, D), f32),
            struct((rows, D), f32),
            struct(w_gu.shape, bf16),
            struct(w_down.shape, bf16),
        ],
        scratch_shapes=[pltpu.VMEM(w_gu.shape, f32), pltpu.VMEM(w_down.shape, f32)],
        compiler_params=params,
        name="feed_forward",
    )(x, cot, w_gu, w_down)


def per_device(
    hidden_in,
    segment_ids,
    out_grad,
    norm_gain,
    w_qkv,
    w_o,
    w_zx,
    w_bc,
    w_dt,
    conv_w,
    conv_b,
    dt_bias,
    a_log,
    d_skip,
    w_out,
    second_gain,
    w_gate_up,
    w_down,
):
    micro, _, tokens, D = hidden_in.shape
    F, C = lax.axis_size("fsdp"), lax.axis_size("ctx")
    c = lax.axis_index("ctx")
    f = lax.axis_index("fsdp")
    length = tokens * C
    rows = micro * length
    mh = MH // C
    qw, dw, fw = QW // C, DI // C, FF // C
    kv = c * KV // C
    dt_pad = 128 - mh

    def cols(weight, start, size):
        return lax.dynamic_slice_in_dim(weight, start, size, 1)

    block = w_qkv.shape[0]
    first_shard = jnp.concatenate(
        [
            cols(w_qkv, c * qw, qw),
            cols(w_qkv, QW + kv * HD, HD),
            cols(w_qkv, QW + KW + kv * HD, HD),
            cols(w_zx, c * dw, dw),
            cols(w_zx, DI + c * dw, dw),
            w_bc,
            cols(w_dt, c * mh, mh),
            jnp.zeros((block, dt_pad), bf16),
        ],
        axis=1,
    )
    gu_shard = jnp.concatenate([cols(w_gate_up, c * fw, fw), cols(w_gate_up, FF + c * fw, fw)], 1)
    ro, rz, rd = w_o.shape[0] // C, w_out.shape[0] // C, w_down.shape[0] // C
    row_shard = jnp.concatenate(
        [
            lax.dynamic_slice_in_dim(w_o, c * ro, ro, 0),
            lax.dynamic_slice_in_dim(w_out, c * rz, rz, 0),
            lax.dynamic_slice_in_dim(w_down, c * rd, rd, 0),
        ],
        axis=0,
    )
    row_shard = to_owner_columns(row_shard, False)
    xb = conv_b.shape[0]
    small_shard = jnp.concatenate(
        [conv_w.reshape(-1), conv_b, norm_gain, second_gain], axis=0
    )
    small_all = pair_gather(small_shard, "fsdp")
    first_column = line_gather(first_shard)
    first_column, row_shard = lax.optimization_barrier((first_column, row_shard))
    row_column = line_gather(row_shard)
    row_column, gu_shard = lax.optimization_barrier((row_column, gu_shard))
    gu_column = line_gather(gu_shard)
    w_first = join_pairs(first_column).reshape(D, -1)
    row_all = join_pairs(row_column)
    w_gu = join_pairs(gu_column).reshape(D, -1)

    conv_all = small_all[:, : (CONV + 1) * xb].reshape(F, CONV + 1, xb)
    conv_all = conv_all.transpose(1, 0, 2).reshape(CONV + 1, XC).astype(f32)
    conv_own = jnp.concatenate([cols(conv_all, c * dw, dw), conv_all[:, DI:]], axis=1)
    gains = small_all[:, (CONV + 1) * xb :].astype(f32)
    gain = gains[:, :block].reshape(1, D)
    gain_two = gains[:, block:].reshape(1, D)
    w_mix = jnp.concatenate(
        [row_all[:, :ro].reshape(F * ro, D), row_all[:, ro : ro + rz].reshape(F * rz, D)], axis=0
    )
    w_down_own = row_all[:, ro + rz :].reshape(F * rd, D)
    dtb = lax.dynamic_slice_in_dim(dt_bias, c * mh, mh, 0)
    a_rate = jnp.exp(lax.dynamic_slice_in_dim(a_log, c * mh, mh, 0))
    skip = lax.dynamic_slice_in_dim(d_skip, c * mh, mh, 0)

    def gather_tokens(own):
        return ctx_gather(own).transpose(1, 0, 2, 3).reshape(rows, D)

    def scatter_tokens(partial):
        return ctx_scatter(partial.reshape(micro, C, tokens, D).transpose(1, 0, 2, 3))

    hidden_own = hidden_in[:, 0].astype(f32)
    hidden = gather_tokens(hidden_in[:, 0])
    cot = gather_tokens(out_grad[:, 0])
    tables = mixer_tables(segment_ids[:, 0], conv_own, dtb, a_rate, skip)

    normed, *saved = mixer_forward(hidden, gain, w_first, tables, micro)
    mixed = dot_plain(saved[-1], w_mix)
    middle = hidden_own + scatter_tokens(mixed)
    second_rms = lax.rsqrt(jnp.mean(middle * middle, axis=-1, keepdims=True) + epsilon)
    second_normed = gather_tokens((middle * second_rms * gain_two).astype(bf16))

    d_second, ffn_out, g_gu, g_down = ffn_both(second_normed, cot, w_gu, w_down_own, micro)
    d_second = scatter_tokens(d_second)
    block_out = (middle + scatter_tokens(ffn_out)).astype(bf16)
    g_gain_two = jnp.sum(d_second * middle * second_rms, axis=(0, 1))
    scaled_two = d_second * gain_two
    d_middle_own = (
        out_grad[:, 0].astype(f32)
        + second_rms * scaled_two
        - middle * second_rms**3 * jnp.mean(middle * scaled_two, axis=-1, keepdims=True)
    ).astype(bf16)
    d_middle = gather_tokens(d_middle_own)
    d_normed_part, g_first, g_mix, g_gain, g_conv, g_head, g_skip = mixer_backward(
        d_middle, hidden, w_first, w_mix, tables, (normed, *saved), micro
    )
    g_gain = g_gain[0]
    g_conv = g_conv[: CONV + 1]
    g_dtb, g_alog = g_head[0, :mh], g_head[1, :mh]
    g_skip = g_skip.reshape(mh, MP).sum(1)
    d_normed = scatter_tokens(d_normed_part)
    inv_own = lax.rsqrt(jnp.mean(hidden_own * hidden_own, axis=-1, keepdims=True) + epsilon)
    scaled = d_normed * gain
    grad_in = (
        d_middle_own.astype(f32)
        + inv_own * scaled
        - hidden_own * inv_own**3 * jnp.mean(hidden_own * scaled, axis=-1, keepdims=True)
    ).astype(bf16)

    ffn = jnp.concatenate([g_gu.reshape(F, block, -1), g_down.reshape(F, rd, D)], axis=1)
    ffn = fsdp_scatter(ffn).astype(bf16)
    width = w_first.shape[1]
    g_o, g_out = g_mix[: F * ro].reshape(F, ro, D), g_mix[F * ro :].reshape(F, rz, D)
    spare = ((0, 0), (0, 0), (0, width - D))
    last = jnp.concatenate(
        [g_first.reshape(F, block, width), jnp.pad(g_o, spare), jnp.pad(g_out, spare)], axis=1
    )
    last = fsdp_scatter(last).astype(bf16)
    first_sum = last[:block]
    mix = last[block:, :D]
    turned = to_owner_columns(jnp.concatenate([mix, ffn[block:]], axis=0), True)
    turned = ctx_gather(turned).astype(f32)
    grad_o = turned[:, :ro].reshape(C * ro, D)
    grad_out = turned[:, ro : ro + rz].reshape(C * rz, D)
    grad_down = turned[:, ro + rz :].reshape(C * rd, D)

    def side(parts):
        return jnp.concatenate([parts[i] for i in range(C)], axis=1)

    gu_all = ctx_gather(ffn[:block]).astype(f32)
    grad_gate_up = jnp.concatenate([side(gu_all[:, :, :fw]), side(gu_all[:, :, fw:])], axis=1)
    first_all = ctx_gather(first_sum).astype(f32)
    at = qw
    kv_pairs = first_all[:, :, at : at + 2 * HD].reshape(KV, C // KV, block, 2 * HD).sum(1)
    grad_qkv = jnp.concatenate(
        [side(first_all[:, :, :qw])]
        + [kv_pairs[j, :, :HD] for j in range(KV)]
        + [kv_pairs[j, :, HD:] for j in range(KV)],
        axis=1,
    )
    at += 2 * HD
    grad_zx = jnp.concatenate(
        [side(first_all[:, :, at : at + dw]), side(first_all[:, :, at + dw : at + 2 * dw])], axis=1
    )
    at += 2 * dw
    grad_bc = first_all[:, :, at : at + 2 * NS].sum(0)
    at += 2 * NS
    grad_dt = side(first_all[:, :, at : at + mh])

    conv_x = lax.dynamic_update_slice(
        jnp.zeros((CONV + 1, DI), f32), g_conv[:, :dw], (0, c * dw)
    )
    conv_full = jnp.concatenate([conv_x, g_conv[:, dw:]], axis=1)
    conv_full = conv_full.reshape(CONV + 1, F, xb).transpose(1, 0, 2).reshape(F, -1)
    small = jnp.concatenate([conv_full, g_gain.reshape(F, block), g_gain_two.reshape(F, block)], 1)
    heads = jnp.stack([g_dtb, g_alog, g_skip])
    heads = lax.dynamic_update_slice(jnp.zeros((3, MH), f32), heads, (0, c * mh))
    total = everywhere_sum(jnp.concatenate([small.reshape(-1), heads.reshape(-1)]))
    small = lax.dynamic_index_in_dim(total[: small.size].reshape(small.shape), f, 0, False)
    heads = total[-3 * MH :].reshape(3, MH)
    conv_sum = small[: (CONV + 1) * xb].reshape(CONV + 1, xb)
    at = (CONV + 1) * xb
    return (
        block_out[:, None],
        grad_in[:, None],
        small[at : at + block],
        grad_qkv,
        grad_o,
        grad_zx,
        grad_bc,
        grad_dt,
        conv_sum[:CONV],
        conv_sum[CONV],
        heads[0],
        heads[1],
        heads[2],
        grad_out,
        small[at + block :],
        grad_gate_up,
        grad_down,
    )


def solution(mesh):
    tokens = P(None, "fsdp", "ctx", None)
    rows = P("fsdp", None)
    return jax.shard_map(
        per_device,
        mesh=mesh,
        in_specs=(
            tokens,
            P(None, "fsdp", None),
            tokens,
            P("fsdp"),
            rows,
            rows,
            rows,
            rows,
            rows,
            P(None, "fsdp"),
            P("fsdp"),
            P(),
            P(),
            P(),
            rows,
            P("fsdp"),
            rows,
            rows,
        ),
        out_specs=(
            tokens,
            tokens,
            P("fsdp"),
            rows,
            rows,
            rows,
            rows,
            rows,
            P(None, "fsdp"),
            P("fsdp"),
            P(),
            P(),
            P(),
            rows,
            P("fsdp"),
            rows,
            rows,
        ),
        check_vma=False,
    )
```

```python
import math

import jax
import jax.numpy as jnp
from jax import lax
from jax.experimental import pallas as pl
from jax.experimental.pallas import tpu as pltpu
from jax.sharding import PartitionSpec as P

HEADS = 8
KV = 2
HD = 64
MH = 24
MP = 64
NS = 128
CONV = 4
FF = 2048
QW = 512
KW = 128
DI = 1536
XC = 1792

epsilon = 1e-05
rope_base = 100000000000.0
f32 = jnp.float32
bf16 = jnp.bfloat16


def dot_plain(left, right):
    return jnp.dot(left, right, preferred_element_type=f32)


def dot_first(left, right):
    return lax.dot_general(left, right, (((0,), (0,)), ((), ())), preferred_element_type=f32)


def dot_last(left, right):
    return lax.dot_general(left, right, (((1,), (1,)), ((), ())), preferred_element_type=f32)


def swap(block, axis, bit):
    devices = range(lax.axis_size(axis))
    return lax.ppermute(block, axis, [(i, i ^ bit) for i in devices])


def pair_gather(block, axis):
    size = lax.axis_size(axis)
    place = lax.axis_index(axis)
    out = block[None]
    bit = size // 2
    while bit:
        other = swap(out, axis, bit)
        low = (place // bit) % 2 == 0
        out = jnp.where(low, jnp.stack([out, other], 1), jnp.stack([other, out], 1))
        out = out.reshape((-1,) + block.shape)
        bit //= 2
    return out


def ctx_gather(block):
    return pair_gather(block, "ctx")


def line_groups():
    half = lax.axis_size("fsdp") // 2
    return [[2 * k + x for k in range(half)] for x in range(2)]


def line_gather(shard):
    return lax.all_gather(shard, "fsdp", axis=0, tiled=False, axis_index_groups=line_groups())


def both_of_pair(shard):
    first = lax.axis_index("fsdp") % 2 == 0
    other = swap(shard, "fsdp", 1)
    return jnp.where(first, jnp.stack([shard, other]), jnp.stack([other, shard]))


def join_pairs(column):
    first = lax.axis_index("fsdp") % 2 == 0
    other = swap(column, "fsdp", 1)
    both = jnp.where(first, jnp.stack([column, other], 1), jnp.stack([other, column], 1))
    return both.reshape((-1,) + column.shape[1:])


def line_scatter(parts):
    return lax.psum_scatter(
        parts, "fsdp", scatter_dimension=0, tiled=False, axis_index_groups=line_groups()
    )


def hop(block, step):
    size = lax.axis_size("fsdp")
    route = [(i, i + 2 * step) for i in range(size) if 0 <= i + 2 * step < size]
    return lax.ppermute(block, "fsdp", route)


def line_scatter_hops(parts):
    size = parts.shape[0]
    if size > 4:
        return line_scatter(parts)
    place = lax.axis_index("fsdp") // 2
    piece = lambda k: lax.dynamic_index_in_dim(parts, k % size, 0, False).astype(f32)
    up = down = 0.0
    for step in range(1, size):
        up = hop((piece(size - step + place) + up).astype(bf16), 1).astype(f32)
        down = hop((piece(step + place) + down).astype(bf16), -1).astype(f32)
    return (piece(place) + up + down).astype(bf16)


def pair_sum(parts, axis):
    mine = lax.axis_index("fsdp") % 2
    keep = lax.dynamic_index_in_dim(parts, mine, axis, False)
    send = lax.dynamic_index_in_dim(parts, 1 - mine, axis, False)
    return (keep.astype(f32) + swap(send, "fsdp", 1).astype(f32)).astype(bf16)


def split_pairs(parts):
    return parts.reshape((-1, 2) + parts.shape[1:])


def ctx_scatter(parts):
    size = lax.axis_size("ctx")
    place = lax.axis_index("ctx")
    bit = 1
    while bit < size:
        mine = (place // bit) % 2
        parts = parts.reshape((-1, 2) + parts.shape[1:])
        keep = lax.dynamic_index_in_dim(parts, mine, 1, False)
        send = lax.dynamic_index_in_dim(parts, 1 - mine, 1, False)
        got = swap(send.astype(bf16), "ctx", bit)
        parts = keep.astype(f32) + got.astype(f32)
        bit *= 2
    return parts[0]


def everywhere_sum(value):
    for axis in ("ctx", "fsdp"):
        bit = 1
        while bit < lax.axis_size(axis):
            value = value + swap(value, axis, bit)
            bit *= 2
    return value


def to_owner_columns(rows, back):
    F, C = lax.axis_size("fsdp"), lax.axis_size("ctx")
    route = []
    for f in range(F):
        for c in range(C):
            pair = (f * C + c, ((f % (F // C)) * C + c) * C + f // (F // C))
            route.append(pair[::-1] if back else pair)
    return lax.ppermute(rows, ("fsdp", "ctx"), route)


def rotary_tables(positions):
    half_width = HD // 2
    exponents = jnp.arange(half_width, dtype=f32) * (2.0 / HD)
    inverse = jnp.exp(-exponents * math.log(rope_base))
    angles = positions[:, None] * inverse[None, :]
    cosine = jnp.concatenate([jnp.cos(angles), jnp.cos(angles)], axis=1)
    sine = jnp.concatenate([jnp.sin(angles), jnp.sin(angles)], axis=1)
    return (cosine, sine)


def mixer_tables(segments, conv_own, dt_bias, a_rate, skip):
    micro, length = segments.shape
    cosine, sine = rotary_tables(jnp.arange(length).astype(f32))
    columns = []
    for distance in range(CONV):
        behind = jnp.pad(segments, ((0, 0), (distance, 0)), constant_values=-1)[:, :length]
        columns.append((behind == segments).astype(f32))
    columns.append(segments.astype(f32))
    col = jnp.pad(jnp.stack(columns, axis=2), ((0, 0), (0, 0), (0, 128 - len(columns))))
    row = jnp.broadcast_to(segments.astype(f32)[:, None, :], (micro, 8, length))
    conv = jnp.pad(conv_own, ((0, 8 - conv_own.shape[0]), (0, 0)))
    heads = dt_bias.shape[0]
    head = jnp.pad(jnp.stack([dt_bias, a_rate]), ((0, 6), (0, 128 - heads)))
    skip = jnp.broadcast_to(skip[:, None], (heads, MP)).reshape(1, heads * MP)
    double = lambda table: jnp.concatenate([table, table], axis=1)
    return col, row, double(cosine), double(sine), conv, head, skip


def lane_index(shape):
    return lax.broadcasted_iota(jnp.int32, shape, 1)


def turn(tile, forward):
    up = pltpu.roll(tile, 128 - HD // 2, 1)
    down = pltpu.roll(tile, HD // 2, 1)
    low = lane_index(tile.shape) % HD < HD // 2
    return jnp.where(low, -up, down) if forward else jnp.where(low, up, -down)


def half_select(first, second):
    return jnp.where(lane_index(first.shape) < HD, first, second)


def half_only(tile, which):
    low = lane_index(tile.shape) < HD
    return jnp.where(low if which == 0 else jnp.logical_not(low), tile, jnp.zeros_like(tile))


def allowed_pairs(col, row):
    length = col.shape[0]
    order_t = lax.broadcasted_iota(jnp.int32, (length, length), 0)
    order_s = lax.broadcasted_iota(jnp.int32, (length, length), 1)
    return (order_s <= order_t) & (col[:, CONV : CONV + 1] == row[0:1, :])


def mixer_state(conv_f, dt_raw, col, conv, head):
    length = conv_f.shape[0]
    behind = [col[:, 0:1] * conv_f]
    for k in range(1, CONV):
        behind.append(col[:, k : k + 1] * pltpu.roll(conv_f, k, 0))
    pre = conv[CONV : CONV + 1, :]
    for k in range(CONV):
        pre = pre + behind[k] * conv[CONV - 1 - k : CONV - k, :]
    step_pre = dt_raw + head[0:1, :]
    step = jnp.maximum(step_pre, 0.0) + jnp.log1p(jnp.exp(-jnp.abs(step_pre)))
    decay_log = -step * head[1:2, :]
    order_t = lax.broadcasted_iota(jnp.int32, (length, length), 0)
    order_s = lax.broadcasted_iota(jnp.int32, (length, length), 1)
    lower = (order_s <= order_t).astype(f32)
    cum = jnp.dot(lower, decay_log, precision=lax.Precision.HIGHEST, preferred_element_type=f32)
    return behind, pre, step_pre, step, decay_log, cum


def decay_kernel(cum, cum_t, valid, h):
    return jnp.exp(jnp.where(valid, cum[:, h : h + 1] - cum_t[h : h + 1, :], -1e30))


def softmax_rows(queries, keys, valid, scale):
    scores = jnp.where(valid, dot_last(queries, keys) * scale, -1e30)
    peak = jnp.max(scores, axis=-1, keepdims=True)
    expo = jnp.exp(scores - peak)
    return expo / jnp.sum(expo, axis=-1, keepdims=True)


def forward_body(
    hidden_ref,
    gain_ref,
    w_ref,
    col_ref,
    row_ref,
    cos_ref,
    sin_ref,
    conv_ref,
    head_ref,
    skip_ref,
    normed_ref,
    qkv_ref,
    gate_ref,
    conv_in_ref,
    dt_ref,
    y_ref,
    mixed_ref,
):
    scale = 1.0 / math.sqrt(HD)
    dw = gate_ref.shape[1]
    heads = dw // MP
    hidden = hidden_ref[...].astype(f32)
    inv_rms = lax.rsqrt(jnp.mean(hidden * hidden, axis=-1, keepdims=True) + epsilon)
    normed = (hidden * inv_rms * gain_ref[...]).astype(bf16)
    normed_ref[...] = normed
    first = dot_plain(normed, w_ref[...])
    col, row = col_ref[0], row_ref[0]
    valid = allowed_pairs(col, row)
    cos, sin = cos_ref[...], sin_ref[...]
    q = first[:, :128]
    q = (q * cos + turn(q, True) * sin).astype(bf16)
    kv = first[:, 128:256]
    kv = half_select(kv * cos + turn(kv, True) * sin, kv)
    qkv_ref[:, :128] = q
    qkv_ref[:, 128:] = kv.astype(bf16)
    kv_turned = pltpu.roll(kv, HD, 1)
    keys = half_select(kv, kv_turned).astype(bf16)
    values = half_select(kv_turned, kv).astype(bf16)
    outs = []
    for h in range(2):
        probability = softmax_rows(half_only(q, h), keys, valid, scale)
        outs.append(dot_plain(probability.astype(bf16), values))
    mixed_ref[:, :128] = half_select(outs[0], outs[1]).astype(bf16)

    gate_z = first[:, 256 : 256 + dw]
    gate_ref[...] = gate_z
    conv_in = first[:, 256 + dw : 256 + 2 * dw + 2 * NS].astype(bf16)
    conv_in_ref[...] = conv_in
    dt_raw = first[:, 256 + 2 * dw + 2 * NS :]
    dt_ref[...] = dt_raw
    _, pre, _, step, _, cum = mixer_state(conv_in.astype(f32), dt_raw, col, conv_ref[...], head_ref[...])
    act = pre * jax.nn.sigmoid(pre)
    cum_t = jnp.transpose(cum)
    b_map = act[:, dw : dw + NS].astype(bf16)
    c_map = act[:, dw + NS :].astype(bf16)
    cross = dot_last(c_map, b_map)
    for j in range(heads // 2):
        x = act[:, 128 * j : 128 * (j + 1)]
        driven = (x * half_select_col(step, 2 * j, x.shape)).astype(bf16)
        pair = []
        for h in (2 * j, 2 * j + 1):
            weighted = decay_kernel(cum, cum_t, valid, h) * cross
            pair.append(dot_plain(weighted.astype(bf16), driven))
        y = half_select(pair[0], pair[1]) + skip_ref[:, 128 * j : 128 * (j + 1)] * x
        y_ref[:, 128 * j : 128 * (j + 1)] = y
        z = gate_z[:, 128 * j : 128 * (j + 1)]
        mixed_ref[:, 128 * (j + 1) : 128 * (j + 2)] = (y * z * jax.nn.sigmoid(z)).astype(bf16)


def half_select_col(columns, h, shape):
    return jnp.where(lane_index(shape) < MP, columns[:, h : h + 1], columns[:, h + 1 : h + 2])


def backward_body(
    d_mid_ref,
    hidden_ref,
    w_ref,
    w_mix_ref,
    col_ref,
    row_ref,
    cos_ref,
    sin_ref,
    conv_ref,
    head_ref,
    skip_ref,
    normed_ref,
    qkv_ref,
    gate_ref,
    conv_in_ref,
    dt_ref,
    y_ref,
    mixed_ref,
    d_normed_ref,
    g_first_ref,
    g_gain_ref,
    g_conv_ref,
    g_head_ref,
    g_skip_ref,
    acc_first,
    d_first,
):
    scale = 1.0 / math.sqrt(HD)
    dw = gate_ref.shape[1]
    heads = dw // MP
    at_conv = 256 + dw
    at_dt = at_conv + dw + 2 * NS
    first_step = pl.program_id(0) == 0

    @pl.when(first_step)
    def _():
        acc_first[...] = jnp.zeros_like(acc_first)
        g_gain_ref[...] = jnp.zeros_like(g_gain_ref)
        g_conv_ref[...] = jnp.zeros_like(g_conv_ref)
        g_head_ref[...] = jnp.zeros_like(g_head_ref)
        g_skip_ref[...] = jnp.zeros_like(g_skip_ref)

    col, row = col_ref[0], row_ref[0]
    valid = allowed_pairs(col, row)
    length = col.shape[0]
    d_mid = d_mid_ref[...]
    d_mixed = dot_last(d_mid, w_mix_ref[...]).astype(bf16)

    cos, sin = cos_ref[...], sin_ref[...]
    q = qkv_ref[:, :128]
    kv = qkv_ref[:, 128:].astype(f32)
    kv_turned = pltpu.roll(kv, HD, 1)
    keys = half_select(kv, kv_turned).astype(bf16)
    values = half_select(kv_turned, kv).astype(bf16)
    d_att = d_mixed[:, :128]
    d_q, d_k, d_v = [], 0.0, 0.0
    for h in range(2):
        q_h = half_only(q, h)
        d_att_h = half_only(d_att, h)
        probability = softmax_rows(q_h, keys, valid, scale)
        d_prob = dot_last(d_att_h, values)
        delta = jnp.sum(probability * d_prob, axis=-1, keepdims=True)
        d_scores = (probability * (d_prob - delta)).astype(bf16)
        d_q.append(dot_plain(d_scores, keys))
        d_k = d_k + dot_first(d_scores, q_h)
        d_v = d_v + dot_first(probability.astype(bf16), d_att_h)
    d_q = half_select(d_q[0], d_q[1]) * scale
    d_k = (d_k + pltpu.roll(d_k, HD, 1)) * scale
    d_v = d_v + pltpu.roll(d_v, HD, 1)
    d_first[:, :128] = (d_q * cos + turn(d_q * sin, False)).astype(bf16)
    d_first[:, 128:256] = half_select(d_k * cos + turn(d_k * sin, False), d_v).astype(bf16)

    conv = conv_ref[...]
    behind, pre, step_pre, step, decay_log, cum = mixer_state(
        conv_in_ref[...].astype(f32), dt_ref[...], col, conv, head_ref[...]
    )
    sig = jax.nn.sigmoid(pre)
    act = pre * sig
    slope = sig * (1.0 + pre * (1.0 - sig))
    cum_t = jnp.transpose(cum)
    b_map = act[:, dw : dw + NS].astype(bf16)
    c_map = act[:, dw + NS :].astype(bf16)
    cross = dot_last(c_map, b_map)
    d_cross = jnp.zeros((length, length), f32)
    lanes = lane_index((length, 128))
    row_sums = jnp.zeros((length, 128), f32)
    x_sums = jnp.zeros((length, 128), f32)
    col_sums = []
    d_x_parts = []
    for j in range(heads // 2):
        part = slice(128 * j, 128 * (j + 1))
        z = gate_ref[:, part]
        z_sig = jax.nn.sigmoid(z)
        d_gated = d_mixed[:, 128 * (j + 1) : 128 * (j + 2)].astype(f32)
        d_first[:, 256 + 128 * j : 256 + 128 * (j + 1)] = (
            d_gated * y_ref[:, part] * (z_sig * (1.0 + z * (1.0 - z_sig)))
        ).astype(bf16)
        d_y = d_gated * (z * z_sig)
        d_y16 = d_y.astype(bf16)
        x = act[:, part]
        step_x = half_select_col(step, 2 * j, x.shape)
        driven = (x * step_x).astype(bf16)
        pair = []
        for h in (2 * j, 2 * j + 1):
            kernel = decay_kernel(cum, cum_t, valid, h)
            weighted = kernel * cross
            d_weighted = dot_last(half_only(d_y16, h - 2 * j), driven)
            d_cross = d_cross + d_weighted * kernel
            pairs = d_weighted * weighted
            row_sums = jnp.where(lanes == h, jnp.sum(pairs, axis=1, keepdims=True), row_sums)
            col_sums.append(jnp.sum(pairs, axis=0, keepdims=True))
            pair.append(dot_first(weighted.astype(bf16), d_y16))
        d_driven = half_select(pair[0], pair[1])
        d_x_parts.append(d_driven * step_x + skip_ref[:, part] * d_y)
        dx = d_driven * x
        for h in (2 * j, 2 * j + 1):
            x_sums = jnp.where(
                lanes == h, jnp.sum(half_only(dx, h - 2 * j), axis=1, keepdims=True), x_sums
            )
        g_skip_ref[:, part] += jnp.sum(d_y * x, axis=0, keepdims=True)
    col_sums = jnp.concatenate(col_sums + [jnp.zeros((128 - heads, length), f32)], axis=0)
    d_cum = row_sums - jnp.transpose(col_sums)
    order_t = lax.broadcasted_iota(jnp.int32, (length, length), 0)
    order_s = lax.broadcasted_iota(jnp.int32, (length, length), 1)
    upper = (order_s >= order_t).astype(f32)
    d_decay = jnp.dot(upper, d_cum, precision=lax.Precision.HIGHEST, preferred_element_type=f32)
    d_dt = (x_sums - d_decay * head_ref[1:2, :]) * jax.nn.sigmoid(step_pre)
    d_first[:, at_dt:] = d_dt.astype(bf16)
    g_head_ref[0:1, :] += jnp.sum(d_dt, axis=0, keepdims=True)
    g_head_ref[1:2, :] += jnp.sum(d_decay * decay_log, axis=0, keepdims=True)
    d_cross16 = d_cross.astype(bf16)
    d_act = d_x_parts + [dot_first(d_cross16, c_map), dot_plain(d_cross16, b_map)]
    for i, piece in enumerate(d_act):
        part = slice(128 * i, 128 * (i + 1))
        d_pre = piece * slope[:, part]
        g_conv_ref[CONV : CONV + 1, part] += jnp.sum(d_pre, axis=0, keepdims=True)
        d_conv = 0.0
        for k in range(CONV):
            tap = CONV - 1 - k
            g_conv_ref[tap : tap + 1, part] += jnp.sum(d_pre * behind[k][:, part], axis=0, keepdims=True)
            moved = col[:, k : k + 1] * d_pre
            if k:
                moved = pltpu.roll(moved, length - k, 0)
            d_conv = d_conv + moved * conv[tap : tap + 1, part]
        d_first[:, at_conv + 128 * i : at_conv + 128 * (i + 1)] = d_conv.astype(bf16)

    d_all = d_first[...]
    d_normed = dot_last(d_all, w_ref[...])
    d_normed_ref[...] = d_normed
    hidden = hidden_ref[...].astype(f32)
    inv_rms = lax.rsqrt(jnp.mean(hidden * hidden, axis=-1, keepdims=True) + epsilon)
    g_gain_ref[...] += jnp.sum(d_normed * (hidden * inv_rms), axis=0, keepdims=True)
    acc_first[...] += dot_first(normed_ref[...], d_all)

    @pl.when(pl.program_id(0) == pl.num_programs(0) - 1)
    def _():
        g_first_ref[...] = acc_first[...].astype(bf16)


def ffn_body(x_ref, cot_ref, gu_ref, down_ref, d_second_ref, out_ref, *rest):
    fw = down_ref.shape[0]
    acc_gu, acc_down = rest[-2:]

    @pl.when(pl.program_id(0) == 0)
    def _():
        acc_gu[...] = jnp.zeros_like(acc_gu)
        acc_down[...] = jnp.zeros_like(acc_down)

    x, cot = x_ref[...], cot_ref[...]
    gate_up = dot_plain(x, gu_ref[...])
    gate, up = gate_up[:, :fw], gate_up[:, fw:]
    sig = jax.nn.sigmoid(gate)
    gate_silu = gate * sig
    d_units = dot_last(cot, down_ref[...]).astype(bf16).astype(f32)
    d_gate = (d_units * up * (sig * (1.0 + gate * (1.0 - sig)))).astype(bf16)
    d_up = (d_units * gate_silu).astype(bf16)
    d_second_ref[...] = dot_last(d_gate, gu_ref[:, :fw]) + dot_last(d_up, gu_ref[:, fw:])
    units = (gate_silu * up).astype(bf16)
    out_ref[...] = dot_plain(units, down_ref[...])
    acc_gu[:, :fw] += dot_first(x, d_gate)
    acc_gu[:, fw:] += dot_first(x, d_up)
    acc_down[...] += dot_first(units, cot)

    @pl.when(pl.program_id(0) == pl.num_programs(0) - 1)
    def _():
        if len(rest) == 4:
            rest[0][...] = acc_gu[...].astype(bf16)
            rest[1][...] = acc_down[...].astype(bf16)
        else:
            parts = rest[0].shape[0]
            block, rd = acc_gu.shape[0] // parts, acc_down.shape[0] // parts
            for i in range(parts):
                rest[0][i, :block] = acc_gu[i * block : (i + 1) * block].astype(bf16)
                rest[0][i, block:] = acc_down[i * rd : (i + 1) * rd].astype(bf16)


def per_pack(block_rows, width):
    return pl.BlockSpec((block_rows, width), lambda m: (m, 0))


def per_pack3(rows, width):
    return pl.BlockSpec((1, rows, width), lambda m: (m, 0, 0))


def whole(shape):
    return pl.BlockSpec(shape, lambda m: (0,) * len(shape))


def struct(shape, kind):
    return jax.ShapeDtypeStruct(shape, kind)


params = pltpu.CompilerParams(
    dimension_semantics=("arbitrary",), vmem_limit_bytes=56 * 1024 * 1024
)


def mixer_forward(hidden, gain, w_first, tables, micro):
    rows, D = hidden.shape
    length = rows // micro
    col, row, cos, sin, conv, head, skip = tables
    dw, width = skip.shape[1], w_first.shape[1]
    cw = conv.shape[1]
    shapes = [(D, bf16), (256, bf16), (dw, f32), (cw, bf16), (128, f32), (dw, f32), (128 + dw, bf16)]
    return pl.pallas_call(
        forward_body,
        grid=(micro,),
        in_specs=[
            per_pack(length, D),
            whole(gain.shape),
            whole(w_first.shape),
            per_pack3(length, 128),
            per_pack3(8, length),
            whole(cos.shape),
            whole(sin.shape),
            whole(conv.shape),
            whole(head.shape),
            whole(skip.shape),
        ],
        out_specs=[per_pack(length, n) for n, _ in shapes],
        out_shape=[struct((rows, n), kind) for n, kind in shapes],
        compiler_params=params,
        name="mixer_forward",
    )(hidden, gain, w_first, col, row, cos, sin, conv, head, skip)


def mixer_backward(d_middle, hidden, w_first, w_mix, tables, saved, micro):
    rows, D = hidden.shape
    length = rows // micro
    col, row, cos, sin, conv, head, skip = tables
    width = w_first.shape[1]
    flat = [whole(a.shape) for a in (cos, sin, conv, head, skip)]
    sums = [w_first.shape, (1, D), conv.shape, head.shape, skip.shape]
    kinds = [bf16, f32, f32, f32, f32]
    return pl.pallas_call(
        backward_body,
        grid=(micro,),
        in_specs=[
            per_pack(length, D),
            per_pack(length, D),
            whole(w_first.shape),
            whole(w_mix.shape),
            per_pack3(length, 128),
            per_pack3(8, length),
        ]
        + flat
        + [per_pack(length, a.shape[1]) for a in saved],
        out_specs=[per_pack(length, D)] + [whole(s) for s in sums],
        out_shape=[struct((rows, D), f32)] + [struct(s, k) for s, k in zip(sums, kinds)],
        scratch_shapes=[
            pltpu.VMEM(w_first.shape, f32),
            pltpu.VMEM((length, width), bf16),
        ],
        compiler_params=params,
        name="mixer_backward",
    )(d_middle, hidden, w_first, w_mix, col, row, cos, sin, conv, head, skip, *saved)


def ffn_both(x, cot, w_gu, w_down, micro, parts):
    rows, D = x.shape
    length = rows // micro
    block, rd = D // parts, w_down.shape[0] // parts
    joined = block % 16 == 0 and rd % 16 == 0
    shapes = [(parts, block + rd, D)] if joined else [w_gu.shape, w_down.shape]
    out = pl.pallas_call(
        ffn_body,
        grid=(micro,),
        in_specs=[per_pack(length, D), per_pack(length, D), whole(w_gu.shape), whole(w_down.shape)],
        out_specs=[per_pack(length, D), per_pack(length, D)] + [whole(s) for s in shapes],
        out_shape=[struct((rows, D), f32), struct((rows, D), f32)]
        + [struct(s, bf16) for s in shapes],
        scratch_shapes=[pltpu.VMEM(w_gu.shape, f32), pltpu.VMEM(w_down.shape, f32)],
        compiler_params=params,
        name="feed_forward",
    )(x, cot, w_gu, w_down)
    if joined:
        return out
    d_second, ffn_out, g_gu, g_down = out
    g_ffn = jnp.concatenate([g_gu.reshape(parts, block, -1), g_down.reshape(parts, rd, D)], axis=1)
    return d_second, ffn_out, g_ffn


def assemble_body(first_ref, qkv_ref, zx_ref, bc_ref, dt_ref):
    size, block, _ = first_ref.shape
    dw = zx_ref.shape[1] // 2 // size
    mh = dt_ref.shape[1] // size
    at_bc = 256 + 2 * dw
    group = size // KV
    heads = []
    for v in range(KV):
        tile = 0.0
        for i in range(v * group, (v + 1) * group):
            tile = tile + first_ref[i, :, 128:256].astype(f32)
        heads.append(tile)
    qkv_ref[:, QW : QW + KW] = half_select(heads[0], pltpu.roll(heads[1], HD, 1))
    qkv_ref[:, QW + KW :] = half_select(pltpu.roll(heads[0], HD, 1), heads[1])
    bc = 0.0
    steps = jnp.zeros((block, 128), f32)
    lanes = lane_index((block, 128))
    for i in range(size):
        qkv_ref[:, 128 * i : 128 * (i + 1)] = first_ref[i, :, :128].astype(f32)
        zx_ref[:, dw * i : dw * (i + 1)] = first_ref[i, :, 256 : 256 + dw].astype(f32)
        zx_ref[:, DI + dw * i : DI + dw * (i + 1)] = first_ref[i, :, 256 + dw : at_bc].astype(f32)
        bc = bc + first_ref[i, :, at_bc : at_bc + 2 * NS].astype(f32)
        tile = first_ref[i, :, at_bc + 2 * NS :].astype(f32)
        if i:
            tile = pltpu.roll(tile, mh * i, 1)
        steps = jnp.where((lanes >= mh * i) & (lanes < mh * (i + 1)), tile, steps)
    bc_ref[...] = bc
    dt_ref[...] = steps[:, : mh * size]


def assemble_first(first_all, widths):
    block = first_all.shape[1]
    return pl.pallas_call(
        assemble_body,
        out_shape=[struct((block, n), f32) for n in widths],
        compiler_params=pltpu.CompilerParams(vmem_limit_bytes=56 * 1024 * 1024),
        name="assemble_first",
    )(first_all)


def per_device(
    hidden_in,
    segment_ids,
    out_grad,
    norm_gain,
    w_qkv,
    w_o,
    w_zx,
    w_bc,
    w_dt,
    conv_w,
    conv_b,
    dt_bias,
    a_log,
    d_skip,
    w_out,
    second_gain,
    w_gate_up,
    w_down,
):
    micro, _, tokens, D = hidden_in.shape
    F, C = lax.axis_size("fsdp"), lax.axis_size("ctx")
    c = lax.axis_index("ctx")
    f = lax.axis_index("fsdp")
    length = tokens * C
    rows = micro * length
    mh = MH // C
    qw, dw, fw = QW // C, DI // C, FF // C
    kv = c * KV // C
    dt_pad = 128 - mh

    def cols(weight, start, size):
        return lax.dynamic_slice_in_dim(weight, start, size, 1)

    block = w_qkv.shape[0]
    first_shard = jnp.concatenate(
        [
            cols(w_qkv, c * qw, qw),
            cols(w_qkv, QW + kv * HD, HD),
            cols(w_qkv, QW + KW + kv * HD, HD),
            cols(w_zx, c * dw, dw),
            cols(w_zx, DI + c * dw, dw),
            w_bc,
            cols(w_dt, c * mh, mh),
            jnp.zeros((block, dt_pad), bf16),
        ],
        axis=1,
    )
    gu_shard = jnp.concatenate([cols(w_gate_up, c * fw, fw), cols(w_gate_up, FF + c * fw, fw)], 1)
    ro, rz, rd = w_o.shape[0] // C, w_out.shape[0] // C, w_down.shape[0] // C
    row_shard = jnp.concatenate(
        [
            lax.dynamic_slice_in_dim(w_o, c * ro, ro, 0),
            lax.dynamic_slice_in_dim(w_out, c * rz, rz, 0),
            lax.dynamic_slice_in_dim(w_down, c * rd, rd, 0),
        ],
        axis=0,
    )
    row_shard = to_owner_columns(row_shard, False)
    xb = conv_b.shape[0]
    small_shard = jnp.concatenate(
        [conv_w.reshape(-1), conv_b, norm_gain, second_gain], axis=0
    )
    small_all = pair_gather(small_shard, "fsdp")
    bar = lax.optimization_barrier
    first_column = line_gather(first_shard)
    first_column, row_shard = bar((first_column, row_shard))
    row_column = line_gather(row_shard)
    row_column, gu_pair = bar((row_column, both_of_pair(gu_shard)))
    w_gu = line_gather(gu_pair).reshape(D, -1)
    w_first = join_pairs(first_column).reshape(D, -1)
    row_all = join_pairs(row_column)

    conv_all = small_all[:, : (CONV + 1) * xb].reshape(F, CONV + 1, xb)
    conv_all = conv_all.transpose(1, 0, 2).reshape(CONV + 1, XC).astype(f32)
    conv_own = jnp.concatenate([cols(conv_all, c * dw, dw), conv_all[:, DI:]], axis=1)
    gains = small_all[:, (CONV + 1) * xb :].astype(f32)
    gain = gains[:, :block].reshape(1, D)
    gain_two = gains[:, block:].reshape(1, D)
    w_mix = jnp.concatenate(
        [row_all[:, :ro].reshape(F * ro, D), row_all[:, ro : ro + rz].reshape(F * rz, D)], axis=0
    )
    w_down_own = row_all[:, ro + rz :].reshape(F * rd, D)
    dtb = lax.dynamic_slice_in_dim(dt_bias, c * mh, mh, 0)
    a_rate = jnp.exp(lax.dynamic_slice_in_dim(a_log, c * mh, mh, 0))
    skip = lax.dynamic_slice_in_dim(d_skip, c * mh, mh, 0)

    def gather_tokens(own):
        return ctx_gather(own).transpose(1, 0, 2, 3).reshape(rows, D)

    def scatter_tokens(partial):
        return ctx_scatter(partial.reshape(micro, C, tokens, D).transpose(1, 0, 2, 3))

    hidden_own = hidden_in[:, 0].astype(f32)
    hidden = gather_tokens(hidden_in[:, 0])
    cot = gather_tokens(out_grad[:, 0])
    tables = mixer_tables(segment_ids[:, 0], conv_own, dtb, a_rate, skip)

    normed, *saved = mixer_forward(hidden, gain, w_first, tables, micro)
    mixed = dot_plain(saved[-1], w_mix)
    middle = hidden_own + scatter_tokens(mixed)
    second_rms = lax.rsqrt(jnp.mean(middle * middle, axis=-1, keepdims=True) + epsilon)
    second_normed = gather_tokens((middle * second_rms * gain_two).astype(bf16))

    d_second, ffn_out, g_ffn = ffn_both(second_normed, cot, w_gu, w_down_own, micro, F)
    d_second = scatter_tokens(d_second)
    block_out = (middle + scatter_tokens(ffn_out)).astype(bf16)
    g_gain_two = jnp.sum(d_second * middle * second_rms, axis=(0, 1))
    scaled_two = d_second * gain_two
    d_middle_own = (
        out_grad[:, 0].astype(f32)
        + second_rms * scaled_two
        - middle * second_rms**3 * jnp.mean(middle * scaled_two, axis=-1, keepdims=True)
    ).astype(bf16)
    d_middle = gather_tokens(d_middle_own)
    g_mix = dot_first(saved[-1], d_middle).astype(bf16)
    d_middle, g_mix = bar((d_middle, g_mix))
    g_o, g_out = g_mix[: F * ro].reshape(F, ro, D), g_mix[F * ro :].reshape(F, rz, D)
    mix_half = pair_sum(split_pairs(jnp.concatenate([g_o, g_out], axis=1)), 1)
    d_normed_part, g_first, g_gain, g_conv, g_head, g_skip = mixer_backward(
        d_middle, hidden, w_first, w_mix, tables, (normed, *saved), micro
    )
    ffn = line_scatter(split_pairs(g_ffn))
    first_half = pair_sum(split_pairs(g_first.reshape(F, block, -1)), 1)
    d_normed = scatter_tokens(d_normed_part)
    g_gain = g_gain[0]
    g_conv = g_conv[: CONV + 1]
    g_dtb, g_alog = g_head[0, :mh], g_head[1, :mh]
    g_skip = g_skip.reshape(mh, MP).sum(1)
    conv_x = lax.dynamic_update_slice(
        jnp.zeros((CONV + 1, DI), f32), g_conv[:, :dw], (0, c * dw)
    )
    conv_full = jnp.concatenate([conv_x, g_conv[:, dw:]], axis=1)
    conv_full = conv_full.reshape(CONV + 1, F, xb).transpose(1, 0, 2).reshape(F, -1)
    small = jnp.concatenate([conv_full, g_gain.reshape(F, block), g_gain_two.reshape(F, block)], 1)
    heads = jnp.stack([g_dtb, g_alog, g_skip])
    heads = lax.dynamic_update_slice(jnp.zeros((3, MH), f32), heads, (0, c * mh))
    total = jnp.concatenate([small.reshape(-1), heads.reshape(-1)])
    mix = line_scatter_hops(mix_half)
    ffn, first_half, mix, d_normed, total = bar((ffn, first_half, mix, d_normed, total))
    first_sum = line_scatter(first_half)
    ffn = pair_sum(ffn, 0)
    total = everywhere_sum(total)
    small = lax.dynamic_index_in_dim(total[: small.size].reshape(small.shape), f, 0, False)
    heads = total[-3 * MH :].reshape(3, MH)
    inv_own = lax.rsqrt(jnp.mean(hidden_own * hidden_own, axis=-1, keepdims=True) + epsilon)
    scaled = d_normed * gain
    grad_in = (
        d_middle_own.astype(f32)
        + inv_own * scaled
        - hidden_own * inv_own**3 * jnp.mean(hidden_own * scaled, axis=-1, keepdims=True)
    ).astype(bf16)

    turned = to_owner_columns(jnp.concatenate([mix, ffn[block:]], axis=0), True)
    turned = ctx_gather(turned).astype(f32)
    grad_o = turned[:, :ro].reshape(C * ro, D)
    grad_out = turned[:, ro : ro + rz].reshape(C * rz, D)
    grad_down = turned[:, ro + rz :].reshape(C * rd, D)

    def side(parts):
        return jnp.concatenate([parts[i] for i in range(C)], axis=1)

    gu_all = ctx_gather(ffn[:block]).astype(f32)
    grad_gate_up = jnp.concatenate([side(gu_all[:, :, :fw]), side(gu_all[:, :, fw:])], axis=1)
    grad_qkv, grad_zx, grad_bc, grad_dt = assemble_first(
        ctx_gather(first_sum), [w_qkv.shape[1], w_zx.shape[1], w_bc.shape[1], w_dt.shape[1]]
    )

    conv_sum = small[: (CONV + 1) * xb].reshape(CONV + 1, xb)
    at = (CONV + 1) * xb
    return (
        block_out[:, None],
        grad_in[:, None],
        small[at : at + block],
        grad_qkv,
        grad_o,
        grad_zx,
        grad_bc,
        grad_dt,
        conv_sum[:CONV],
        conv_sum[CONV],
        heads[0],
        heads[1],
        heads[2],
        grad_out,
        small[at + block :],
        grad_gate_up,
        grad_down,
    )


def solution(mesh):
    tokens = P(None, "fsdp", "ctx", None)
    rows = P("fsdp", None)
    return jax.shard_map(
        per_device,
        mesh=mesh,
        in_specs=(
            tokens,
            P(None, "fsdp", None),
            tokens,
            P("fsdp"),
            rows,
            rows,
            rows,
            rows,
            rows,
            P(None, "fsdp"),
            P("fsdp"),
            P(),
            P(),
            P(),
            rows,
            P("fsdp"),
            rows,
            rows,
        ),
        out_specs=(
            tokens,
            tokens,
            P("fsdp"),
            rows,
            rows,
            rows,
            rows,
            rows,
            P(None, "fsdp"),
            P("fsdp"),
            P(),
            P(),
            P(),
            rows,
            P("fsdp"),
            rows,
            rows,
        ),
        check_vma=False,
    )
```

```python
import math

import jax
import jax.numpy as jnp
from jax import lax
from jax.experimental import pallas as pl
from jax.experimental.pallas import tpu as pltpu
from jax.sharding import PartitionSpec as P

HEADS = 8
KV = 2
HD = 64
MH = 24
MP = 64
NS = 128
CONV = 4
FF = 2048
QW = 512
KW = 128
DI = 1536
XC = 1792

epsilon = 1e-05
rope_base = 100000000000.0
f32 = jnp.float32
bf16 = jnp.bfloat16


def dot_plain(left, right):
    return jnp.dot(left, right, preferred_element_type=f32)


def dot_first(left, right):
    return lax.dot_general(left, right, (((0,), (0,)), ((), ())), preferred_element_type=f32)


def dot_last(left, right):
    return lax.dot_general(left, right, (((1,), (1,)), ((), ())), preferred_element_type=f32)


def swap(block, axis, bit):
    devices = range(lax.axis_size(axis))
    return lax.ppermute(block, axis, [(i, i ^ bit) for i in devices])


def pair_gather(block, axis):
    size = lax.axis_size(axis)
    place = lax.axis_index(axis)
    out = block[None]
    bit = size // 2
    while bit:
        other = swap(out, axis, bit)
        low = (place // bit) % 2 == 0
        out = jnp.where(low, jnp.stack([out, other], 1), jnp.stack([other, out], 1))
        out = out.reshape((-1,) + block.shape)
        bit //= 2
    return out


def ctx_gather(block):
    return pair_gather(block, "ctx")


def line_groups():
    half = lax.axis_size("fsdp") // 2
    return [[2 * k + x for k in range(half)] for x in range(2)]


def line_gather(shard):
    return lax.all_gather(shard, "fsdp", axis=0, tiled=False, axis_index_groups=line_groups())


def both_of_pair(shard):
    first = lax.axis_index("fsdp") % 2 == 0
    other = swap(shard, "fsdp", 1)
    return jnp.where(first, jnp.stack([shard, other]), jnp.stack([other, shard]))


def join_pairs(column):
    first = lax.axis_index("fsdp") % 2 == 0
    other = swap(column, "fsdp", 1)
    both = jnp.where(first, jnp.stack([column, other], 1), jnp.stack([other, column], 1))
    return both.reshape((-1,) + column.shape[1:])


def line_scatter(parts):
    return lax.psum_scatter(
        parts, "fsdp", scatter_dimension=0, tiled=False, axis_index_groups=line_groups()
    )


def hop(block, step):
    size = lax.axis_size("fsdp")
    route = [(i, i + 2 * step) for i in range(size) if 0 <= i + 2 * step < size]
    return lax.ppermute(block, "fsdp", route)


def line_scatter_hops(parts):
    size = parts.shape[0]
    if size > 4:
        return line_scatter(parts)
    place = lax.axis_index("fsdp") // 2
    piece = lambda k: lax.dynamic_index_in_dim(parts, k % size, 0, False).astype(f32)
    up = down = 0.0
    for step in range(1, size):
        up = hop((piece(size - step + place) + up).astype(bf16), 1).astype(f32)
        down = hop((piece(step + place) + down).astype(bf16), -1).astype(f32)
    return (piece(place) + up + down).astype(bf16)


def pair_sum(parts, axis):
    mine = lax.axis_index("fsdp") % 2
    keep = lax.dynamic_index_in_dim(parts, mine, axis, False)
    send = lax.dynamic_index_in_dim(parts, 1 - mine, axis, False)
    return (keep.astype(f32) + swap(send, "fsdp", 1).astype(f32)).astype(bf16)


def split_pairs(parts):
    return parts.reshape((-1, 2) + parts.shape[1:])


def ctx_scatter(parts):
    size = lax.axis_size("ctx")
    place = lax.axis_index("ctx")
    bit = 1
    while bit < size:
        mine = (place // bit) % 2
        parts = parts.reshape((-1, 2) + parts.shape[1:])
        keep = lax.dynamic_index_in_dim(parts, mine, 1, False)
        send = lax.dynamic_index_in_dim(parts, 1 - mine, 1, False)
        got = swap(send.astype(bf16), "ctx", bit)
        parts = keep.astype(f32) + got.astype(f32)
        bit *= 2
    return parts[0]


def everywhere_sum(value):
    for axis in ("ctx", "fsdp"):
        bit = 1
        while bit < lax.axis_size(axis):
            value = value + swap(value, axis, bit)
            bit *= 2
    return value


def to_owner_columns(rows, back):
    F, C = lax.axis_size("fsdp"), lax.axis_size("ctx")
    route = []
    for f in range(F):
        for c in range(C):
            pair = (f * C + c, ((f % (F // C)) * C + c) * C + f // (F // C))
            route.append(pair[::-1] if back else pair)
    return lax.ppermute(rows, ("fsdp", "ctx"), route)


def rotary_tables(positions):
    half_width = HD // 2
    exponents = jnp.arange(half_width, dtype=f32) * (2.0 / HD)
    inverse = jnp.exp(-exponents * math.log(rope_base))
    angles = positions[:, None] * inverse[None, :]
    cosine = jnp.concatenate([jnp.cos(angles), jnp.cos(angles)], axis=1)
    sine = jnp.concatenate([jnp.sin(angles), jnp.sin(angles)], axis=1)
    return (cosine, sine)


def mixer_tables(segments, conv_own, dt_bias, a_rate, skip):
    micro, length = segments.shape
    cosine, sine = rotary_tables(jnp.arange(length).astype(f32))
    columns = []
    for distance in range(CONV):
        behind = jnp.pad(segments, ((0, 0), (distance, 0)), constant_values=-1)[:, :length]
        columns.append((behind == segments).astype(f32))
    columns.append(segments.astype(f32))
    col = jnp.pad(jnp.stack(columns, axis=2), ((0, 0), (0, 0), (0, 128 - len(columns))))
    row = jnp.broadcast_to(segments.astype(f32)[:, None, :], (micro, 8, length))
    conv = jnp.pad(conv_own, ((0, 8 - conv_own.shape[0]), (0, 0)))
    heads = dt_bias.shape[0]
    head = jnp.pad(jnp.stack([dt_bias, a_rate]), ((0, 6), (0, 128 - heads)))
    skip = jnp.broadcast_to(skip[:, None], (heads, MP)).reshape(1, heads * MP)
    double = lambda table: jnp.concatenate([table, table], axis=1)
    return col, row, double(cosine), double(sine), conv, head, skip


def lane_index(shape):
    return lax.broadcasted_iota(jnp.int32, shape, 1)


def turn(tile, forward):
    up = pltpu.roll(tile, 128 - HD // 2, 1)
    down = pltpu.roll(tile, HD // 2, 1)
    low = lane_index(tile.shape) % HD < HD // 2
    return jnp.where(low, -up, down) if forward else jnp.where(low, up, -down)


def half_select(first, second):
    return jnp.where(lane_index(first.shape) < HD, first, second)


def half_only(tile, which):
    low = lane_index(tile.shape) < HD
    return jnp.where(low if which == 0 else jnp.logical_not(low), tile, jnp.zeros_like(tile))


def allowed_pairs(col, row):
    length = col.shape[0]
    order_t = lax.broadcasted_iota(jnp.int32, (length, length), 0)
    order_s = lax.broadcasted_iota(jnp.int32, (length, length), 1)
    return (order_s <= order_t) & (col[:, CONV : CONV + 1] == row[0:1, :])


def mixer_state(conv_f, dt_raw, col, conv, head):
    length = conv_f.shape[0]
    behind = [col[:, 0:1] * conv_f]
    for k in range(1, CONV):
        behind.append(col[:, k : k + 1] * pltpu.roll(conv_f, k, 0))
    pre = conv[CONV : CONV + 1, :]
    for k in range(CONV):
        pre = pre + behind[k] * conv[CONV - 1 - k : CONV - k, :]
    step_pre = dt_raw + head[0:1, :]
    step = jnp.maximum(step_pre, 0.0) + jnp.log1p(jnp.exp(-jnp.abs(step_pre)))
    decay_log = -step * head[1:2, :]
    order_t = lax.broadcasted_iota(jnp.int32, (length, length), 0)
    order_s = lax.broadcasted_iota(jnp.int32, (length, length), 1)
    lower = (order_s <= order_t).astype(f32)
    cum = jnp.dot(lower, decay_log, precision=lax.Precision.HIGHEST, preferred_element_type=f32)
    return behind, pre, step_pre, step, decay_log, cum


def decay_kernel(cum, cum_t, valid, h):
    return jnp.exp(jnp.where(valid, cum[:, h : h + 1] - cum_t[h : h + 1, :], -1e30))


def softmax_rows(queries, keys, valid, scale):
    scores = jnp.where(valid, dot_last(queries, keys) * scale, -1e30)
    peak = jnp.max(scores, axis=-1, keepdims=True)
    expo = jnp.exp(scores - peak)
    return expo / jnp.sum(expo, axis=-1, keepdims=True)


def forward_body(
    hidden_ref,
    gain_ref,
    w_ref,
    col_ref,
    row_ref,
    cos_ref,
    sin_ref,
    conv_ref,
    head_ref,
    skip_ref,
    normed_ref,
    qkv_ref,
    gate_ref,
    conv_in_ref,
    dt_ref,
    y_ref,
    mixed_ref,
):
    scale = 1.0 / math.sqrt(HD)
    dw = gate_ref.shape[1]
    heads = dw // MP
    hidden = hidden_ref[...].astype(f32)
    inv_rms = lax.rsqrt(jnp.mean(hidden * hidden, axis=-1, keepdims=True) + epsilon)
    normed = (hidden * inv_rms * gain_ref[...]).astype(bf16)
    normed_ref[...] = normed
    first = dot_plain(normed, w_ref[...])
    col, row = col_ref[0], row_ref[0]
    valid = allowed_pairs(col, row)
    cos, sin = cos_ref[...], sin_ref[...]
    q = first[:, :128]
    q = (q * cos + turn(q, True) * sin).astype(bf16)
    kv = first[:, 128:256]
    kv = half_select(kv * cos + turn(kv, True) * sin, kv)
    qkv_ref[:, :128] = q
    qkv_ref[:, 128:] = kv.astype(bf16)
    kv_turned = pltpu.roll(kv, HD, 1)
    keys = half_select(kv, kv_turned).astype(bf16)
    values = half_select(kv_turned, kv).astype(bf16)
    outs = []
    for h in range(2):
        probability = softmax_rows(half_only(q, h), keys, valid, scale)
        outs.append(dot_plain(probability.astype(bf16), values))
    mixed_ref[:, :128] = half_select(outs[0], outs[1]).astype(bf16)

    gate_z = first[:, 256 : 256 + dw]
    gate_ref[...] = gate_z
    conv_in = first[:, 256 + dw : 256 + 2 * dw + 2 * NS].astype(bf16)
    conv_in_ref[...] = conv_in
    dt_raw = first[:, 256 + 2 * dw + 2 * NS :]
    dt_ref[...] = dt_raw
    _, pre, _, step, _, cum = mixer_state(conv_in.astype(f32), dt_raw, col, conv_ref[...], head_ref[...])
    act = pre * jax.nn.sigmoid(pre)
    cum_t = jnp.transpose(cum)
    b_map = act[:, dw : dw + NS].astype(bf16)
    c_map = act[:, dw + NS :].astype(bf16)
    cross = dot_last(c_map, b_map)
    for j in range(heads // 2):
        x = act[:, 128 * j : 128 * (j + 1)]
        driven = (x * half_select_col(step, 2 * j, x.shape)).astype(bf16)
        pair = []
        for h in (2 * j, 2 * j + 1):
            weighted = decay_kernel(cum, cum_t, valid, h) * cross
            pair.append(dot_plain(weighted.astype(bf16), driven))
        y = half_select(pair[0], pair[1]) + skip_ref[:, 128 * j : 128 * (j + 1)] * x
        y_ref[:, 128 * j : 128 * (j + 1)] = y
        z = gate_z[:, 128 * j : 128 * (j + 1)]
        mixed_ref[:, 128 * (j + 1) : 128 * (j + 2)] = (y * z * jax.nn.sigmoid(z)).astype(bf16)


def half_select_col(columns, h, shape):
    return jnp.where(lane_index(shape) < MP, columns[:, h : h + 1], columns[:, h + 1 : h + 2])


def backward_body(
    d_mid_ref,
    hidden_ref,
    w_ref,
    w_mix_ref,
    col_ref,
    row_ref,
    cos_ref,
    sin_ref,
    conv_ref,
    head_ref,
    skip_ref,
    normed_ref,
    qkv_ref,
    gate_ref,
    conv_in_ref,
    dt_ref,
    y_ref,
    mixed_ref,
    d_normed_ref,
    g_first_ref,
    g_gain_ref,
    g_conv_ref,
    g_head_ref,
    g_skip_ref,
    acc_first,
    d_first,
):
    scale = 1.0 / math.sqrt(HD)
    dw = gate_ref.shape[1]
    heads = dw // MP
    at_conv = 256 + dw
    at_dt = at_conv + dw + 2 * NS
    first_step = pl.program_id(0) == 0

    @pl.when(first_step)
    def _():
        acc_first[...] = jnp.zeros_like(acc_first)
        g_gain_ref[...] = jnp.zeros_like(g_gain_ref)
        g_conv_ref[...] = jnp.zeros_like(g_conv_ref)
        g_head_ref[...] = jnp.zeros_like(g_head_ref)
        g_skip_ref[...] = jnp.zeros_like(g_skip_ref)

    col, row = col_ref[0], row_ref[0]
    valid = allowed_pairs(col, row)
    length = col.shape[0]
    d_mid = d_mid_ref[...]
    d_mixed = dot_last(d_mid, w_mix_ref[...]).astype(bf16)

    cos, sin = cos_ref[...], sin_ref[...]
    q = qkv_ref[:, :128]
    kv = qkv_ref[:, 128:].astype(f32)
    kv_turned = pltpu.roll(kv, HD, 1)
    keys = half_select(kv, kv_turned).astype(bf16)
    values = half_select(kv_turned, kv).astype(bf16)
    d_att = d_mixed[:, :128]
    d_q, d_k, d_v = [], 0.0, 0.0
    for h in range(2):
        q_h = half_only(q, h)
        d_att_h = half_only(d_att, h)
        probability = softmax_rows(q_h, keys, valid, scale)
        d_prob = dot_last(d_att_h, values)
        delta = jnp.sum(probability * d_prob, axis=-1, keepdims=True)
        d_scores = (probability * (d_prob - delta)).astype(bf16)
        d_q.append(dot_plain(d_scores, keys))
        d_k = d_k + dot_first(d_scores, q_h)
        d_v = d_v + dot_first(probability.astype(bf16), d_att_h)
    d_q = half_select(d_q[0], d_q[1]) * scale
    d_k = (d_k + pltpu.roll(d_k, HD, 1)) * scale
    d_v = d_v + pltpu.roll(d_v, HD, 1)
    d_first[:, :128] = (d_q * cos + turn(d_q * sin, False)).astype(bf16)
    d_first[:, 128:256] = half_select(d_k * cos + turn(d_k * sin, False), d_v).astype(bf16)

    conv = conv_ref[...]
    behind, pre, step_pre, step, decay_log, cum = mixer_state(
        conv_in_ref[...].astype(f32), dt_ref[...], col, conv, head_ref[...]
    )
    sig = jax.nn.sigmoid(pre)
    act = pre * sig
    slope = sig * (1.0 + pre * (1.0 - sig))
    cum_t = jnp.transpose(cum)
    b_map = act[:, dw : dw + NS].astype(bf16)
    c_map = act[:, dw + NS :].astype(bf16)
    cross = dot_last(c_map, b_map)
    d_cross = jnp.zeros((length, length), f32)
    lanes = lane_index((length, 128))
    row_sums = jnp.zeros((length, 128), f32)
    x_sums = jnp.zeros((length, 128), f32)
    col_sums = []
    d_x_parts = []
    for j in range(heads // 2):
        part = slice(128 * j, 128 * (j + 1))
        z = gate_ref[:, part]
        z_sig = jax.nn.sigmoid(z)
        d_gated = d_mixed[:, 128 * (j + 1) : 128 * (j + 2)].astype(f32)
        d_first[:, 256 + 128 * j : 256 + 128 * (j + 1)] = (
            d_gated * y_ref[:, part] * (z_sig * (1.0 + z * (1.0 - z_sig)))
        ).astype(bf16)
        d_y = d_gated * (z * z_sig)
        d_y16 = d_y.astype(bf16)
        x = act[:, part]
        step_x = half_select_col(step, 2 * j, x.shape)
        driven = (x * step_x).astype(bf16)
        pair = []
        for h in (2 * j, 2 * j + 1):
            kernel = decay_kernel(cum, cum_t, valid, h)
            weighted = kernel * cross
            d_weighted = dot_last(half_only(d_y16, h - 2 * j), driven)
            d_cross = d_cross + d_weighted * kernel
            pairs = d_weighted * weighted
            row_sums = jnp.where(lanes == h, jnp.sum(pairs, axis=1, keepdims=True), row_sums)
            col_sums.append(jnp.sum(pairs, axis=0, keepdims=True))
            pair.append(dot_first(weighted.astype(bf16), d_y16))
        d_driven = half_select(pair[0], pair[1])
        d_x_parts.append(d_driven * step_x + skip_ref[:, part] * d_y)
        dx = d_driven * x
        for h in (2 * j, 2 * j + 1):
            x_sums = jnp.where(
                lanes == h, jnp.sum(half_only(dx, h - 2 * j), axis=1, keepdims=True), x_sums
            )
        g_skip_ref[:, part] += jnp.sum(d_y * x, axis=0, keepdims=True)
    col_sums = jnp.concatenate(col_sums + [jnp.zeros((128 - heads, length), f32)], axis=0)
    d_cum = row_sums - jnp.transpose(col_sums)
    order_t = lax.broadcasted_iota(jnp.int32, (length, length), 0)
    order_s = lax.broadcasted_iota(jnp.int32, (length, length), 1)
    upper = (order_s >= order_t).astype(f32)
    d_decay = jnp.dot(upper, d_cum, precision=lax.Precision.HIGHEST, preferred_element_type=f32)
    d_dt = (x_sums - d_decay * head_ref[1:2, :]) * jax.nn.sigmoid(step_pre)
    d_first[:, at_dt:] = d_dt.astype(bf16)
    g_head_ref[0:1, :] += jnp.sum(d_dt, axis=0, keepdims=True)
    g_head_ref[1:2, :] += jnp.sum(d_decay * decay_log, axis=0, keepdims=True)
    d_cross16 = d_cross.astype(bf16)
    d_act = d_x_parts + [dot_first(d_cross16, c_map), dot_plain(d_cross16, b_map)]
    for i, piece in enumerate(d_act):
        part = slice(128 * i, 128 * (i + 1))
        d_pre = piece * slope[:, part]
        g_conv_ref[CONV : CONV + 1, part] += jnp.sum(d_pre, axis=0, keepdims=True)
        d_conv = 0.0
        for k in range(CONV):
            tap = CONV - 1 - k
            g_conv_ref[tap : tap + 1, part] += jnp.sum(d_pre * behind[k][:, part], axis=0, keepdims=True)
            moved = col[:, k : k + 1] * d_pre
            if k:
                moved = pltpu.roll(moved, length - k, 0)
            d_conv = d_conv + moved * conv[tap : tap + 1, part]
        d_first[:, at_conv + 128 * i : at_conv + 128 * (i + 1)] = d_conv.astype(bf16)

    d_all = d_first[...]
    d_normed = dot_last(d_all, w_ref[...])
    d_normed_ref[...] = d_normed
    hidden = hidden_ref[...].astype(f32)
    inv_rms = lax.rsqrt(jnp.mean(hidden * hidden, axis=-1, keepdims=True) + epsilon)
    g_gain_ref[...] += jnp.sum(d_normed * (hidden * inv_rms), axis=0, keepdims=True)
    acc_first[...] += dot_first(normed_ref[...], d_all)

    @pl.when(pl.program_id(0) == pl.num_programs(0) - 1)
    def _():
        g_first_ref[...] = acc_first[...].astype(bf16)


def ffn_body(x_ref, cot_ref, gu_ref, down_ref, d_second_ref, out_ref, *rest):
    fw = down_ref.shape[0]
    acc_gu, acc_down = rest[-2:]

    @pl.when(pl.program_id(0) == 0)
    def _():
        acc_gu[...] = jnp.zeros_like(acc_gu)
        acc_down[...] = jnp.zeros_like(acc_down)

    x, cot = x_ref[...], cot_ref[...]
    gate_up = dot_plain(x, gu_ref[...])
    gate, up = gate_up[:, :fw], gate_up[:, fw:]
    sig = jax.nn.sigmoid(gate)
    gate_silu = gate * sig
    d_units = dot_last(cot, down_ref[...]).astype(bf16).astype(f32)
    d_gate = (d_units * up * (sig * (1.0 + gate * (1.0 - sig)))).astype(bf16)
    d_up = (d_units * gate_silu).astype(bf16)
    d_second_ref[...] = dot_last(d_gate, gu_ref[:, :fw]) + dot_last(d_up, gu_ref[:, fw:])
    units = (gate_silu * up).astype(bf16)
    out_ref[...] = dot_plain(units, down_ref[...])
    acc_gu[:, :fw] += dot_first(x, d_gate)
    acc_gu[:, fw:] += dot_first(x, d_up)
    acc_down[...] += dot_first(units, cot)

    @pl.when(pl.program_id(0) == pl.num_programs(0) - 1)
    def _():
        if len(rest) == 4:
            rest[0][...] = acc_gu[...].astype(bf16)
            rest[1][...] = acc_down[...].astype(bf16)
        else:
            parts = rest[0].shape[0]
            block, rd = acc_gu.shape[0] // parts, acc_down.shape[0] // parts
            for i in range(parts):
                rest[0][i, :block] = acc_gu[i * block : (i + 1) * block].astype(bf16)
                rest[0][i, block:] = acc_down[i * rd : (i + 1) * rd].astype(bf16)


def per_pack(block_rows, width):
    return pl.BlockSpec((block_rows, width), lambda m: (m, 0))


def per_pack3(rows, width):
    return pl.BlockSpec((1, rows, width), lambda m: (m, 0, 0))


def whole(shape):
    return pl.BlockSpec(shape, lambda m: (0,) * len(shape))


def struct(shape, kind):
    return jax.ShapeDtypeStruct(shape, kind)


params = pltpu.CompilerParams(
    dimension_semantics=("arbitrary",), vmem_limit_bytes=56 * 1024 * 1024
)


def mixer_forward(hidden, gain, w_first, tables, micro):
    rows, D = hidden.shape
    length = rows // micro
    col, row, cos, sin, conv, head, skip = tables
    dw, width = skip.shape[1], w_first.shape[1]
    cw = conv.shape[1]
    shapes = [(D, bf16), (256, bf16), (dw, f32), (cw, bf16), (128, f32), (dw, f32), (128 + dw, bf16)]
    return pl.pallas_call(
        forward_body,
        grid=(micro,),
        in_specs=[
            per_pack(length, D),
            whole(gain.shape),
            whole(w_first.shape),
            per_pack3(length, 128),
            per_pack3(8, length),
            whole(cos.shape),
            whole(sin.shape),
            whole(conv.shape),
            whole(head.shape),
            whole(skip.shape),
        ],
        out_specs=[per_pack(length, n) for n, _ in shapes],
        out_shape=[struct((rows, n), kind) for n, kind in shapes],
        compiler_params=params,
        name="mixer_forward",
    )(hidden, gain, w_first, col, row, cos, sin, conv, head, skip)


def mixer_backward(d_middle, hidden, w_first, w_mix, tables, saved, micro):
    rows, D = hidden.shape
    length = rows // micro
    col, row, cos, sin, conv, head, skip = tables
    width = w_first.shape[1]
    flat = [whole(a.shape) for a in (cos, sin, conv, head, skip)]
    sums = [w_first.shape, (1, D), conv.shape, head.shape, skip.shape]
    kinds = [bf16, f32, f32, f32, f32]
    return pl.pallas_call(
        backward_body,
        grid=(micro,),
        in_specs=[
            per_pack(length, D),
            per_pack(length, D),
            whole(w_first.shape),
            whole(w_mix.shape),
            per_pack3(length, 128),
            per_pack3(8, length),
        ]
        + flat
        + [per_pack(length, a.shape[1]) for a in saved],
        out_specs=[per_pack(length, D)] + [whole(s) for s in sums],
        out_shape=[struct((rows, D), f32)] + [struct(s, k) for s, k in zip(sums, kinds)],
        scratch_shapes=[
            pltpu.VMEM(w_first.shape, f32),
            pltpu.VMEM((length, width), bf16),
        ],
        compiler_params=params,
        name="mixer_backward",
    )(d_middle, hidden, w_first, w_mix, col, row, cos, sin, conv, head, skip, *saved)


def ffn_both(x, cot, w_gu, w_down, micro, parts):
    rows, D = x.shape
    length = rows // micro
    block, rd = D // parts, w_down.shape[0] // parts
    joined = block % 16 == 0 and rd % 16 == 0
    shapes = [(parts, block + rd, D)] if joined else [w_gu.shape, w_down.shape]
    out = pl.pallas_call(
        ffn_body,
        grid=(micro,),
        in_specs=[per_pack(length, D), per_pack(length, D), whole(w_gu.shape), whole(w_down.shape)],
        out_specs=[per_pack(length, D), per_pack(length, D)] + [whole(s) for s in shapes],
        out_shape=[struct((rows, D), f32), struct((rows, D), f32)]
        + [struct(s, bf16) for s in shapes],
        scratch_shapes=[pltpu.VMEM(w_gu.shape, f32), pltpu.VMEM(w_down.shape, f32)],
        compiler_params=params,
        name="feed_forward",
    )(x, cot, w_gu, w_down)
    if joined:
        return out
    d_second, ffn_out, g_gu, g_down = out
    g_ffn = jnp.concatenate([g_gu.reshape(parts, block, -1), g_down.reshape(parts, rd, D)], axis=1)
    return d_second, ffn_out, g_ffn


def assemble_body(first_ref, qkv_ref, zx_ref, bc_ref, dt_ref):
    size, block, _ = first_ref.shape
    dw = zx_ref.shape[1] // 2 // size
    mh = dt_ref.shape[1] // size
    at_bc = 256 + 2 * dw
    group = size // KV
    heads = []
    for v in range(KV):
        tile = 0.0
        for i in range(v * group, (v + 1) * group):
            tile = tile + first_ref[i, :, 128:256].astype(f32)
        heads.append(tile)
    qkv_ref[:, QW : QW + KW] = half_select(heads[0], pltpu.roll(heads[1], HD, 1))
    qkv_ref[:, QW + KW :] = half_select(pltpu.roll(heads[0], HD, 1), heads[1])
    bc = 0.0
    steps = jnp.zeros((block, 128), f32)
    lanes = lane_index((block, 128))
    for i in range(size):
        qkv_ref[:, 128 * i : 128 * (i + 1)] = first_ref[i, :, :128].astype(f32)
        zx_ref[:, dw * i : dw * (i + 1)] = first_ref[i, :, 256 : 256 + dw].astype(f32)
        zx_ref[:, DI + dw * i : DI + dw * (i + 1)] = first_ref[i, :, 256 + dw : at_bc].astype(f32)
        bc = bc + first_ref[i, :, at_bc : at_bc + 2 * NS].astype(f32)
        tile = first_ref[i, :, at_bc + 2 * NS :].astype(f32)
        if i:
            tile = pltpu.roll(tile, mh * i, 1)
        steps = jnp.where((lanes >= mh * i) & (lanes < mh * (i + 1)), tile, steps)
    bc_ref[...] = bc
    dt_ref[...] = steps[:, : mh * size]


def assemble_first(first_all, widths):
    block = first_all.shape[1]
    return pl.pallas_call(
        assemble_body,
        out_shape=[struct((block, n), f32) for n in widths],
        compiler_params=pltpu.CompilerParams(vmem_limit_bytes=56 * 1024 * 1024),
        name="assemble_first",
    )(first_all)


def per_device(
    hidden_in,
    segment_ids,
    out_grad,
    norm_gain,
    w_qkv,
    w_o,
    w_zx,
    w_bc,
    w_dt,
    conv_w,
    conv_b,
    dt_bias,
    a_log,
    d_skip,
    w_out,
    second_gain,
    w_gate_up,
    w_down,
):
    micro, _, tokens, D = hidden_in.shape
    F, C = lax.axis_size("fsdp"), lax.axis_size("ctx")
    c = lax.axis_index("ctx")
    f = lax.axis_index("fsdp")
    length = tokens * C
    rows = micro * length
    mh = MH // C
    qw, dw, fw = QW // C, DI // C, FF // C
    kv = c * KV // C
    dt_pad = 128 - mh

    def cols(weight, start, size):
        return lax.dynamic_slice_in_dim(weight, start, size, 1)

    block = w_qkv.shape[0]
    first_shard = jnp.concatenate(
        [
            cols(w_qkv, c * qw, qw),
            cols(w_qkv, QW + kv * HD, HD),
            cols(w_qkv, QW + KW + kv * HD, HD),
            cols(w_zx, c * dw, dw),
            cols(w_zx, DI + c * dw, dw),
            w_bc,
            cols(w_dt, c * mh, mh),
            jnp.zeros((block, dt_pad), bf16),
        ],
        axis=1,
    )
    gu_shard = jnp.concatenate([cols(w_gate_up, c * fw, fw), cols(w_gate_up, FF + c * fw, fw)], 1)
    ro, rz, rd = w_o.shape[0] // C, w_out.shape[0] // C, w_down.shape[0] // C
    row_shard = jnp.concatenate(
        [
            lax.dynamic_slice_in_dim(w_o, c * ro, ro, 0),
            lax.dynamic_slice_in_dim(w_out, c * rz, rz, 0),
            lax.dynamic_slice_in_dim(w_down, c * rd, rd, 0),
        ],
        axis=0,
    )
    row_shard = to_owner_columns(row_shard, False)
    xb = conv_b.shape[0]
    small_shard = jnp.concatenate(
        [conv_w.reshape(-1), conv_b, norm_gain, second_gain], axis=0
    )
    small_all = pair_gather(small_shard, "fsdp")
    bar = lax.optimization_barrier
    first_column = line_gather(first_shard)
    first_column, row_shard = bar((first_column, row_shard))
    row_column = line_gather(row_shard)
    row_column, gu_pair = bar((row_column, both_of_pair(gu_shard)))
    w_gu = line_gather(gu_pair).reshape(D, -1)
    w_first = join_pairs(first_column).reshape(D, -1)
    row_all = join_pairs(row_column)

    conv_all = small_all[:, : (CONV + 1) * xb].reshape(F, CONV + 1, xb)
    conv_all = conv_all.transpose(1, 0, 2).reshape(CONV + 1, XC).astype(f32)
    conv_own = jnp.concatenate([cols(conv_all, c * dw, dw), conv_all[:, DI:]], axis=1)
    gains = small_all[:, (CONV + 1) * xb :].astype(f32)
    gain = gains[:, :block].reshape(1, D)
    gain_two = gains[:, block:].reshape(1, D)
    w_mix = jnp.concatenate(
        [row_all[:, :ro].reshape(F * ro, D), row_all[:, ro : ro + rz].reshape(F * rz, D)], axis=0
    )
    w_down_own = row_all[:, ro + rz :].reshape(F * rd, D)
    dtb = lax.dynamic_slice_in_dim(dt_bias, c * mh, mh, 0)
    a_rate = jnp.exp(lax.dynamic_slice_in_dim(a_log, c * mh, mh, 0))
    skip = lax.dynamic_slice_in_dim(d_skip, c * mh, mh, 0)

    def gather_tokens(own):
        return ctx_gather(own).transpose(1, 0, 2, 3).reshape(rows, D)

    def scatter_tokens(partial):
        return ctx_scatter(partial.reshape(micro, C, tokens, D).transpose(1, 0, 2, 3))

    hidden_own = hidden_in[:, 0].astype(f32)
    hidden = gather_tokens(hidden_in[:, 0])
    cot = gather_tokens(out_grad[:, 0])
    tables = mixer_tables(segment_ids[:, 0], conv_own, dtb, a_rate, skip)

    normed, *saved = mixer_forward(hidden, gain, w_first, tables, micro)
    mixed = dot_plain(saved[-1], w_mix)
    middle = hidden_own + scatter_tokens(mixed)
    second_rms = lax.rsqrt(jnp.mean(middle * middle, axis=-1, keepdims=True) + epsilon)
    second_own = (middle * second_rms * gain_two).astype(bf16)
    second_own, w_gu = bar((second_own, w_gu))
    second_normed = gather_tokens(second_own)

    d_second, ffn_out, g_ffn = ffn_both(second_normed, cot, w_gu, w_down_own, micro, F)
    d_second = scatter_tokens(d_second)
    g_gain_two = jnp.sum(d_second * middle * second_rms, axis=(0, 1))
    scaled_two = d_second * gain_two
    d_middle_own = (
        out_grad[:, 0].astype(f32)
        + second_rms * scaled_two
        - middle * second_rms**3 * jnp.mean(middle * scaled_two, axis=-1, keepdims=True)
    ).astype(bf16)
    d_middle = gather_tokens(d_middle_own)
    g_mix = dot_first(saved[-1], d_middle).astype(bf16)
    d_middle, g_mix = bar((d_middle, g_mix))
    g_o, g_out = g_mix[: F * ro].reshape(F, ro, D), g_mix[F * ro :].reshape(F, rz, D)
    mix_half = pair_sum(split_pairs(jnp.concatenate([g_o, g_out], axis=1)), 1)
    d_normed_part, g_first, g_gain, g_conv, g_head, g_skip = mixer_backward(
        d_middle, hidden, w_first, w_mix, tables, (normed, *saved), micro
    )
    ffn = line_scatter(split_pairs(g_ffn))
    first_half = pair_sum(split_pairs(g_first.reshape(F, block, -1)), 1)
    d_normed = scatter_tokens(d_normed_part)
    g_gain = g_gain[0]
    g_conv = g_conv[: CONV + 1]
    g_dtb, g_alog = g_head[0, :mh], g_head[1, :mh]
    g_skip = g_skip.reshape(mh, MP).sum(1)
    conv_x = lax.dynamic_update_slice(
        jnp.zeros((CONV + 1, DI), f32), g_conv[:, :dw], (0, c * dw)
    )
    conv_full = jnp.concatenate([conv_x, g_conv[:, dw:]], axis=1)
    conv_full = conv_full.reshape(CONV + 1, F, xb).transpose(1, 0, 2).reshape(F, -1)
    small = jnp.concatenate([conv_full, g_gain.reshape(F, block), g_gain_two.reshape(F, block)], 1)
    heads = jnp.stack([g_dtb, g_alog, g_skip])
    heads = lax.dynamic_update_slice(jnp.zeros((3, MH), f32), heads, (0, c * mh))
    total = jnp.concatenate([small.reshape(-1), heads.reshape(-1)])
    mix = line_scatter_hops(mix_half)
    ffn, first_half, mix, d_normed, total, ffn_out = bar(
        (ffn, first_half, mix, d_normed, total, ffn_out)
    )
    block_out = (middle + scatter_tokens(ffn_out)).astype(bf16)
    first_sum = line_scatter(first_half)
    ffn = pair_sum(ffn, 0)
    total = everywhere_sum(total)
    small = lax.dynamic_index_in_dim(total[: small.size].reshape(small.shape), f, 0, False)
    heads = total[-3 * MH :].reshape(3, MH)
    inv_own = lax.rsqrt(jnp.mean(hidden_own * hidden_own, axis=-1, keepdims=True) + epsilon)
    scaled = d_normed * gain
    grad_in = (
        d_middle_own.astype(f32)
        + inv_own * scaled
        - hidden_own * inv_own**3 * jnp.mean(hidden_own * scaled, axis=-1, keepdims=True)
    ).astype(bf16)

    turned = to_owner_columns(jnp.concatenate([mix, ffn[block:]], axis=0), True)
    turned = ctx_gather(turned).astype(f32)
    grad_o = turned[:, :ro].reshape(C * ro, D)
    grad_out = turned[:, ro : ro + rz].reshape(C * rz, D)
    grad_down = turned[:, ro + rz :].reshape(C * rd, D)

    def side(parts):
        return jnp.concatenate([parts[i] for i in range(C)], axis=1)

    gu_all = ctx_gather(ffn[:block]).astype(f32)
    grad_gate_up = jnp.concatenate([side(gu_all[:, :, :fw]), side(gu_all[:, :, fw:])], axis=1)
    grad_qkv, grad_zx, grad_bc, grad_dt = assemble_first(
        ctx_gather(first_sum), [w_qkv.shape[1], w_zx.shape[1], w_bc.shape[1], w_dt.shape[1]]
    )

    conv_sum = small[: (CONV + 1) * xb].reshape(CONV + 1, xb)
    at = (CONV + 1) * xb
    return (
        block_out[:, None],
        grad_in[:, None],
        small[at : at + block],
        grad_qkv,
        grad_o,
        grad_zx,
        grad_bc,
        grad_dt,
        conv_sum[:CONV],
        conv_sum[CONV],
        heads[0],
        heads[1],
        heads[2],
        grad_out,
        small[at + block :],
        grad_gate_up,
        grad_down,
    )


def solution(mesh):
    tokens = P(None, "fsdp", "ctx", None)
    rows = P("fsdp", None)
    return jax.shard_map(
        per_device,
        mesh=mesh,
        in_specs=(
            tokens,
            P(None, "fsdp", None),
            tokens,
            P("fsdp"),
            rows,
            rows,
            rows,
            rows,
            rows,
            P(None, "fsdp"),
            P("fsdp"),
            P(),
            P(),
            P(),
            rows,
            P("fsdp"),
            rows,
            rows,
        ),
        out_specs=(
            tokens,
            tokens,
            P("fsdp"),
            rows,
            rows,
            rows,
            rows,
            rows,
            P(None, "fsdp"),
            P("fsdp"),
            P(),
            P(),
            P(),
            rows,
            P("fsdp"),
            rows,
            rows,
        ),
        check_vma=False,
    )
```
